32 devices in a mesh: row: 2 (over y), col: 16 (over z, x, core).
Axes of the slice: x: 2, y: 2, z: 4, core: 2. Of those that a mesh axis runs over, the one named last changes fastest.
Arguments:
- left_emb: float32 [2, 1536, 400], P('row', 'col'), may hold values from -2 to 2
- left_state: float32 [2, 1536], P('row', 'col'), may hold values from 0.001 to 1
- right_emb: float32 [16, 512, 400], P('col', 'row'), may hold values from -2 to 2
- right_state: float32 [16, 512], P('col', 'row'), may hold values from 0.001 to 1
- relation: float32 [64, 400], replicated, may hold values from -2 to 2
- rel_state: float32 [64], replicated, may hold values from 0.001 to 1
- left_ids: int32 [2, 16, 4000], P('row', 'col'), may hold values from 0 to 1535
- rel_ids: int32 [2, 16, 4000], P('row', 'col'), may hold values from 0 to 63
- right_ids: int32 [2, 16, 4000], P('row', 'col'), may hold values from 0 to 511
- neg_ids: int32 [2, 16, 4, 1000], P('row', 'col'), may hold values from 0 to 511
- counts: int32 [2, 16], P('row', 'col'), may hold values from 2000 to 4000, as said below
Outputs:
- new_left: float32 [2, 1536, 400], P('row', 'col')
- new_left_state: float32 [2, 1536], P('row', 'col')
- new_right: float32 [16, 512, 400], P('col', 'row')
- new_right_state: float32 [16, 512], P('col', 'row')
- new_rel: float32 [64, 400], replicated
- new_rel_state: float32 [64], replicated
The draws below stay inside these ranges and needn't reach their ends.
Inputs may be any that keep to these rules, and one draw needn't show every extreme that they name: `counts`: slots at or beyond a bucket's count are padding. Some bucket is full and some bucket holds exactly 2000 edges in every draw.
All inputs are finite; a program needn't handle non-finite values.
Results may differ from the reference program's by a relative error of at most 0.0003.
The reference program's roundings to bfloat16 on the way (of `left_part`, `right_part`, `queries` and `probability`) count: a program that leaves them out, or rounds other values in their place, can miss the bound.
Values may be sent and summed in bfloat16 or wider, within the bound.
No kernel may reach another device: no remote copies, remote signals or barrier semaphores. Data moves between devices by JAX's collectives and lax.ppermute only.
A program may use at most 128 MiB of HBM per device.

```python
import math
import jax
import jax.numpy as jnp
import numpy as np
from jax import lax

D = 400
CH = 1000
NEG = 1000
GROUPS = 4
NREL = 64
PL = 1536
PR = 512
CAP = 4000
N_ROW = 2
N_COL = 16


def draw_left_emb(key, part):
    key = jax.random.fold_in(key, 1)
    noise = jnp.clip(jax.random.normal(key, (N_ROW, PL, D), jnp.float32), -4.0, 4.0)
    return 0.5 * noise


def draw_right_emb(key, part):
    key = jax.random.fold_in(key, 3)
    noise = jnp.clip(jax.random.normal(key, (N_COL, PR, D), jnp.float32), -4.0, 4.0)
    return 0.5 * noise


def draw_relation(key, part):
    key = jax.random.fold_in(key, 5)
    noise = jnp.clip(jax.random.normal(key, (NREL, D), jnp.float32), -4.0, 4.0)
    return 0.5 * noise


def draw_counts(key, part):
    key = jax.random.fold_in(key, 7)
    load_key, pick_key = jax.random.split(key, 2)
    loads = jax.random.randint(load_key, (N_ROW * N_COL,), CAP // 2, CAP + 1)
    order = jax.random.permutation(pick_key, N_ROW * N_COL)
    loads = loads.at[order[0]].set(CAP)
    loads = loads.at[order[1]].set(CAP // 2)
    return loads.reshape(N_ROW, N_COL).astype(jnp.int32)


def plant(result, own_key, least, high):
    extent = result.shape
    index_at = [jax.random.randint(jax.random.fold_in(own_key, axis), (), 0, extent[axis]) for axis in range(len(extent))]
    result = result.at[tuple(index_at)].set(least)
    longest = extent.index(max(extent))
    index_at[longest] = (index_at[longest] + 1) % extent[longest]
    return result.at[tuple(index_at)].set(high)


def shard_levels(own_key, shape, shards, least, largest):
    loudness, own = 1.0, jax.random.fold_in(own_key, 6)
    for position, blocks in shards:
        heights = jnp.exp(jax.random.uniform(jax.random.fold_in(own, position), (blocks,), jnp.float32, least / len(shards), largest / len(shards)))
        loudness = loudness * jnp.repeat(heights, shape[position] // blocks).reshape([-1 if axis == position else 1 for axis in range(len(shape))])
    return loudness


def rank_table(count, lean):
    weights = [(1 << 20) // math.isqrt(grade ** lean) + 1 for grade in range(1, count + 1)]
    deviation = 1 + sum(weights) // (1 << 30)
    return np.cumsum(np.array([max(1, weight // deviation) for weight in weights]))


def ranked(key, shape, count, skew):
    table = rank_table(count, skew)
    ticket = jax.random.randint(jax.random.fold_in(key, 1), shape, 0, int(table[count - 1]))
    standing = jnp.searchsorted(jnp.asarray(table, jnp.int32), ticket, side="right")
    return jax.random.permutation(jax.random.fold_in(key, 2), count)[standing].astype(jnp.int32)


def setup_inputs(seed: int = 0) -> dict:
    key_of = jax.random.split(jax.random.key(seed), 12)
    left_emb = draw_left_emb(jax.random.fold_in(key_of[11], 71), 0)
    left_state = jnp.clip(jnp.exp(math.log(1.0) - 6.9077552 * jax.random.uniform(key_of[1], (N_ROW, PL), jnp.float32) ** shard_levels(key_of[1], (N_ROW, PL), ((0, 2), (1, 16)), -0.2, 0.2)), 0.001, 1.0)
    right_emb = draw_right_emb(jax.random.fold_in(key_of[11], 71), 0)
    right_state = jnp.clip(jnp.exp(math.log(1.0) - 6.9077552 * jax.random.uniform(key_of[3], (N_COL, PR), jnp.float32) ** shard_levels(key_of[3], (N_COL, PR), ((0, 16), (1, 2)), -0.2, 0.2)), 0.001, 1.0)
    relation = draw_relation(jax.random.fold_in(key_of[11], 71), 0)
    rel_state = jnp.clip(jnp.exp(jax.random.uniform(key_of[5], (NREL,), jnp.float32, math.log(0.001), math.log(1.0))), 0.001, 1.0)
    left_ids = plant(ranked(key_of[6], (N_ROW, N_COL, CAP), PL, 2), jax.random.fold_in(key_of[6], 3), 0, PL - 1).astype(jnp.int32)
    rel_ids = plant(jax.random.randint(key_of[7], (N_ROW, N_COL, CAP), 0, NREL), jax.random.fold_in(key_of[7], 1), 0, NREL - 1).astype(jnp.int32)
    right_ids = plant(ranked(key_of[8], (N_ROW, N_COL, CAP), PR, 2), jax.random.fold_in(key_of[8], 3), 0, PR - 1).astype(jnp.int32)
    neg_ids = plant(jax.random.randint(key_of[9], (N_ROW, N_COL, GROUPS, NEG), 0, PR), jax.random.fold_in(key_of[9], 1), 0, PR - 1).astype(jnp.int32)
    counts = draw_counts(jax.random.fold_in(key_of[11], 71), 0)
    return dict(left_emb=left_emb, left_state=left_state, right_emb=right_emb, right_state=right_state, relation=relation, rel_state=rel_state, left_ids=left_ids, rel_ids=rel_ids, right_ids=right_ids, neg_ids=neg_ids, counts=counts)


learn_rate = 0.1
epsilon = 1e-10

def complex_mul(first, second):
    half_width = first.shape[-1] // 2
    first_re, first_im = (first[..., :half_width], first[..., half_width:])
    second_re, second_im = (second[..., :half_width], second[..., half_width:])
    return jnp.concatenate([first_re * second_re - first_im * second_im, first_re * second_im + first_im * second_re], axis=-1)

def complex_back(upstream, other):
    half_width = upstream.shape[-1] // 2
    up_re, up_im = (upstream[..., :half_width], upstream[..., half_width:])
    other_re, other_im = (other[..., :half_width], other[..., half_width:])
    return jnp.concatenate([up_re * other_re + up_im * other_im, up_im * other_re - up_re * other_im], axis=-1)

def group_update(gradients, left_part, right_part, relation, left_slots, rel_slots, right_slots, neg_slots, valid_rows):
    grad_left, grad_right, grad_rel = gradients
    left_vec = left_part[left_slots].astype(jnp.float32)
    rel_vec = relation[rel_slots]
    target = right_part[right_slots]
    negative = right_part[neg_slots]
    queries = complex_mul(left_vec, rel_vec).astype(jnp.bfloat16)
    scores = jnp.dot(queries, negative.T, preferred_element_type=jnp.float32)
    positive = lax.optimization_barrier(jnp.sum(queries.astype(jnp.float32) * target.astype(jnp.float32), axis=-1))
    highest = jnp.maximum(lax.optimization_barrier(jnp.max(scores, axis=-1)), positive)
    expo = jnp.exp(scores - highest[:, None])
    expo_pos = jnp.exp(positive - highest)
    totals = expo_pos + lax.optimization_barrier(jnp.sum(expo, axis=-1))
    mask_value = valid_rows.astype(jnp.float32)
    probability = (expo * (mask_value / totals)[:, None]).astype(jnp.bfloat16)
    pos_coeff = (expo_pos / totals - 1.0) * mask_value
    d_query = pos_coeff[:, None] * target.astype(jnp.float32) + jnp.dot(probability, negative, preferred_element_type=jnp.float32)
    d_negative = jnp.dot(probability.T, queries, preferred_element_type=jnp.float32)
    d_target = pos_coeff[:, None] * queries.astype(jnp.float32)
    d_left = complex_back(d_query, rel_vec)
    d_rel = complex_back(d_query, left_vec)
    grad_left = grad_left.at[left_slots].add(d_left)
    grad_right = grad_right.at[right_slots].add(d_target).at[neg_slots].add(d_negative)
    grad_rel = grad_rel.at[rel_slots].add(d_rel)
    return (grad_left, grad_right, grad_rel)

def row_adagrad(embedding, accumulator, gradient):
    new_accum = accumulator + lax.optimization_barrier(jnp.mean(gradient * gradient, axis=-1))
    return (embedding - learn_rate * gradient / (jnp.sqrt(new_accum)[..., None] + epsilon), new_accum)

def reference(left_emb, left_state, right_emb, right_state, relation, rel_state, left_ids, rel_ids, right_ids, neg_ids, counts):
    left_part = left_emb.astype(jnp.bfloat16)
    right_part = right_emb.astype(jnp.bfloat16)
    width = relation.shape[1]

    def bucket(carry, index):
        row_index = index // N_COL
        col_index = index % N_COL
        left_block = left_part[row_index]
        right_block = right_part[col_index]
        edge_count = counts[row_index, col_index]
        gradients = (jnp.zeros((PL, width), jnp.float32), jnp.zeros((PR, width), jnp.float32), jnp.zeros((NREL, width), jnp.float32))
        for group_index in range(GROUPS):
            group_start = group_index * CH
            left_slots = left_ids[row_index, col_index, group_start:group_start + CH]
            rel_slots = rel_ids[row_index, col_index, group_start:group_start + CH]
            right_slots = right_ids[row_index, col_index, group_start:group_start + CH]
            neg_slots = neg_ids[row_index, col_index, group_index]
            valid_rows = group_start + jnp.arange(CH, dtype=jnp.int32) < edge_count

            def active(current, left_slots=left_slots, rel_slots=rel_slots, right_slots=right_slots, neg_slots=neg_slots, valid_rows=valid_rows):
                return group_update(current, left_block, right_block, relation, left_slots, rel_slots, right_slots, neg_slots, valid_rows)

            def skipped(current):
                return current
            gradients = lax.cond(group_start < edge_count, active, skipped, gradients)
        all_left, all_right, all_rel = carry
        all_left = all_left.at[row_index].add(gradients[0])
        all_right = all_right.at[col_index].add(gradients[1])
        all_rel = all_rel + gradients[2]
        return ((all_left, all_right, all_rel), None)
    start_carry = (jnp.zeros((N_ROW, PL, width), jnp.float32), jnp.zeros((N_COL, PR, width), jnp.float32), jnp.zeros((NREL, width), jnp.float32))
    (grad_left, grad_right, grad_rel), _ = lax.scan(bucket, start_carry, jnp.arange(N_ROW * N_COL, dtype=jnp.int32))
    new_left, new_left_state = row_adagrad(left_emb, left_state, grad_left)
    new_right, new_right_state = row_adagrad(right_emb, right_state, grad_right)
    new_rel, new_rel_state = row_adagrad(relation, rel_state, grad_rel)
    return (new_left, new_left_state, new_right, new_right_state, new_rel, new_rel_state)
```

```python
import functools

import jax
import jax.numpy as jnp
from jax import lax
from jax.experimental import pallas as pl
from jax.experimental.pallas import tpu as pltpu
from jax.sharding import PartitionSpec as P

CH = 1000
LANES = 128
TILE = 256

learn_rate = 0.1
epsilon = 1e-10
bf16 = jnp.bfloat16
f32 = jnp.float32


def round_up(value, step):
    return (value + step - 1) // step * step


def to_halves(array, half_pad):
    half = array.shape[-1] // 2
    pad = [(0, 0)] * (array.ndim - 1) + [(0, half_pad - half)]
    return jnp.concatenate([jnp.pad(array[..., :half], pad), jnp.pad(array[..., half:], pad)], axis=-1)


def from_halves(array, width):
    half_pad = array.shape[-1] // 2
    return jnp.concatenate([array[..., : width // 2], array[..., half_pad : half_pad + width // 2]], axis=-1)


def bits_of(size):
    return [1 << b for b in range(size.bit_length() - 1)]


def swap(array, axis, size, bit):
    return lax.ppermute(array, axis, [(i, i ^ bit) for i in range(size)])


def gather_chunks(array, axis, size):
    for bit in reversed(bits_of(size)):
        array = jnp.concatenate([array, swap(array, axis, size, bit)], axis=0)
    return array


def reduce_chunks(array, axis, size):
    for bit in bits_of(size):
        half = array.shape[0] // 2
        array = array[:half] + swap(array[half:], axis, size, bit)
    return array


def relative_ids(ids, axis, size, share):
    owner = ids // share
    within = ids - owner * share
    apart = owner ^ lax.axis_index(axis)
    place = jnp.zeros_like(apart)
    top = size.bit_length() - 2
    for b in range(top + 1):
        place = place | (((apart >> b) & 1) << (top - b))
    return place * share + within


def split_two(value):
    high = value.astype(bf16)
    return high, (value - high.astype(f32)).astype(bf16)


def dot(a, b):
    return jnp.dot(a, b, preferred_element_type=f32)


def edge_kernel(
    count_ref, ids_ref, mult_ref, left_ref, right_ref, rel_ref,
    query_ref, c_hi_ref, c_lo_ref, d_hi_ref, d_lo_ref, grad_rel_ref,
    rel_parts, right_t,
):
    step = pl.program_id(0)
    tile = ids_ref.shape[2]
    tiles_in_group = pl.num_programs(0) // mult_ref.shape[0]
    n_rel, wide = rel_ref.shape
    half = wide // 2
    n_left, n_right = left_ref.shape[0], right_ref.shape[0]
    rel_rows = rel_parts.shape[0]

    @pl.when(step == 0)
    def _():
        grad_rel_ref[...] = jnp.zeros_like(grad_rel_ref)
        rel_parts[...] = jnp.zeros_like(rel_parts)
        rest = rel_ref[...]
        for part in range(3):
            piece = rest.astype(bf16)
            rel_parts[part * n_rel : (part + 1) * n_rel, :] = piece
            rest = rest - piece.astype(f32)
        right_t[...] = right_ref[...].T

    group = step // tiles_in_group
    start = group * CH + (step - group * tiles_in_group) * tile

    @pl.when(start >= count_ref[0])
    def _():
        for ref in (query_ref, c_hi_ref, c_lo_ref, d_hi_ref, d_lo_ref):
            ref[...] = jnp.zeros_like(ref)

    @pl.when(start < count_ref[0])
    def _():
        ids = ids_ref[0]
        cols = ids.T
        left_col, rel_col, right_col = cols[:, 0:1], cols[:, 1:2], cols[:, 2:3]
        valid = cols[:, 3:4].astype(f32)
        rel_iota = lax.broadcasted_iota(jnp.int32, (tile, rel_rows), 1) % n_rel
        rel_hot = jnp.where(rel_iota == rel_col, 1.0, 0.0).astype(bf16)
        rel_vec = dot(rel_hot, rel_parts[...])
        left_iota = lax.broadcasted_iota(jnp.int32, (tile, n_left), 1)
        left_hot = jnp.where(left_iota == left_col, 1.0, 0.0).astype(bf16)
        left_vec = dot(left_hot, left_ref[...])
        a_re, a_im = left_vec[:, :half], left_vec[:, half:]
        b_re, b_im = rel_vec[:, :half], rel_vec[:, half:]
        query = jnp.concatenate([a_re * b_re - a_im * b_im, a_re * b_im + a_im * b_re], axis=1).astype(bf16)
        query_ref[...] = query
        scores = dot(query, right_t[...])
        mult = mult_ref[group]
        right_iota = lax.broadcasted_iota(jnp.int32, (tile, n_right), 1)
        is_target = right_iota == right_col
        positive = jnp.sum(jnp.where(is_target, scores, 0.0), axis=1, keepdims=True)
        masked = jnp.where(mult > 0.0, scores, -jnp.inf)
        highest = jnp.maximum(jnp.max(masked, axis=1, keepdims=True), positive)
        expo = jnp.exp(masked - highest)
        expo_pos = jnp.exp(positive - highest)
        totals = expo_pos + jnp.sum(expo * mult, axis=1, keepdims=True)
        probability = (expo * (valid / totals)).astype(bf16)
        pos_coeff = (expo_pos / totals - 1.0) * valid
        coeff = mult * probability.astype(f32) + jnp.where(is_target, pos_coeff, 0.0)
        c_hi, c_lo = split_two(coeff)
        c_hi_ref[...] = c_hi
        c_lo_ref[...] = c_lo
        d_query = dot(c_hi, right_ref[...]) + dot(c_lo, right_ref[...])
        g_re, g_im = d_query[:, :half], d_query[:, half:]
        d_left = jnp.concatenate([g_re * b_re + g_im * b_im, g_im * b_re - g_re * b_im], axis=1)
        d_hi, d_lo = split_two(d_left)
        d_hi_ref[...] = d_hi
        d_lo_ref[...] = d_lo
        d_rel = jnp.concatenate([g_re * a_re + g_im * a_im, g_im * a_re - g_re * a_im], axis=1)
        r_hi, r_lo = split_two(d_rel)
        row_iota = lax.broadcasted_iota(jnp.int32, (n_rel, tile), 0)
        rel_hot_t = jnp.where(row_iota == ids[1:2, :], 1.0, 0.0).astype(bf16)
        grad_rel_ref[...] += dot(rel_hot_t, r_hi) + dot(rel_hot_t, r_lo)


def left_kernel(groups_ref, ids_ref, d_hi_ref, d_lo_ref, out_ref):
    rows = out_ref.shape[0]
    edges = ids_ref.shape[2]
    out_ref[...] = jnp.zeros_like(out_ref)
    row_iota = lax.broadcasted_iota(jnp.int32, (rows, edges), 0) + pl.program_id(0) * rows

    def group_step(g, carry):
        hot = jnp.where(row_iota == ids_ref[g, 0:1, :], 1.0, 0.0).astype(bf16)
        here = pl.ds(pl.multiple_of(g * edges, edges), edges)
        out_ref[...] += dot(hot, d_hi_ref[here, :]) + dot(hot, d_lo_ref[here, :])
        return carry

    lax.fori_loop(0, groups_ref[0], group_step, 0)


def right_kernel(query_ref, c_hi_ref, c_lo_ref, out_ref, total):
    step = pl.program_id(0)

    @pl.when(step == 0)
    def _():
        total[...] = jnp.zeros_like(total)

    dims = (((0,), (0,)), ((), ()))
    query = query_ref[...]
    total[...] += lax.dot_general(query, c_hi_ref[...], dims, preferred_element_type=f32) + lax.dot_general(
        query, c_lo_ref[...], dims, preferred_element_type=f32
    )

    @pl.when(step == pl.num_programs(0) - 1)
    def _():
        out_ref[...] = total[...].T


def whole(shape):
    return pl.BlockSpec(shape, lambda *_: (0,) * len(shape))


def body(n_row, n_col, left_emb, left_state, right_emb, right_state, relation, rel_state, left_ids, rel_ids, right_ids, neg_ids, counts):
    width = relation.shape[1]
    half_pad = round_up(width // 2, LANES)
    wide = 2 * half_pad
    left_share, right_share = left_emb.shape[1], right_emb.shape[1]
    n_left, n_right, n_rel = left_share * n_col, right_share * n_row, relation.shape[0]
    groups = neg_ids.shape[2]
    edges = round_up(CH, TILE)
    slots = groups * edges
    tiles = edges // TILE

    right_part = gather_chunks(to_halves(right_emb[0].astype(bf16), half_pad), "row", n_row)
    left_part = gather_chunks(to_halves(left_emb[0].astype(bf16), half_pad), "col", n_col)
    edge_count = counts[0, 0]
    my_left = relative_ids(left_ids[0, 0], "col", n_col, left_share).reshape(groups, CH)
    my_right = relative_ids(right_ids[0, 0], "row", n_row, right_share).reshape(groups, CH)
    my_neg = relative_ids(neg_ids[0, 0], "row", n_row, right_share)
    my_rel = rel_ids[0, 0].reshape(groups, CH)
    valid = (jnp.arange(groups * CH, dtype=jnp.int32) < edge_count).astype(jnp.int32).reshape(groups, CH)
    ids = jnp.stack([my_left, my_rel, my_right, valid] + [jnp.zeros_like(valid)] * 4, axis=1)
    ids = jnp.pad(ids, ((0, 0), (0, 0), (0, edges - CH)))
    hot = jnp.arange(n_right, dtype=jnp.int32)[None, :, None] == my_neg[:, None, :]
    mult = jnp.sum(hot.astype(f32), axis=2)[:, None, :]
    count_arg = edge_count.reshape(1)
    group_arg = (count_arg + CH - 1) // CH

    smem = pl.BlockSpec(memory_space=pltpu.SMEM)
    tile_block = lambda lanes: pl.BlockSpec((TILE, lanes), lambda i: (i, 0))
    query, c_hi, c_lo, d_hi, d_lo, grad_rel = pl.pallas_call(
        edge_kernel,
        grid=(groups * tiles,),
        in_specs=[
            smem,
            pl.BlockSpec((1, 8, TILE), lambda i: (i // tiles, 0, i % tiles)),
            whole((groups, 1, n_right)),
            whole((n_left, wide)),
            whole((n_right, wide)),
            whole((n_rel, wide)),
        ],
        out_specs=[
            tile_block(wide),
            tile_block(n_right),
            tile_block(n_right),
            tile_block(wide),
            tile_block(wide),
            whole((n_rel, wide)),
        ],
        out_shape=[
            jax.ShapeDtypeStruct((slots, wide), bf16),
            jax.ShapeDtypeStruct((slots, n_right), bf16),
            jax.ShapeDtypeStruct((slots, n_right), bf16),
            jax.ShapeDtypeStruct((slots, wide), bf16),
            jax.ShapeDtypeStruct((slots, wide), bf16),
            jax.ShapeDtypeStruct((n_rel, wide), f32),
        ],
        scratch_shapes=[
            pltpu.VMEM((round_up(3 * n_rel, LANES), wide), bf16),
            pltpu.VMEM((wide, n_right), bf16),
        ],
        compiler_params=pltpu.CompilerParams(vmem_limit_bytes=48 << 20),
        name="edges",
    )(count_arg, ids, mult, left_part, right_part, to_halves(relation, half_pad))

    row_block = 256 if n_left % 256 == 0 else left_share
    grad_left = pl.pallas_call(
        left_kernel,
        grid=(n_left // row_block,),
        in_specs=[smem, whole((groups, 8, edges)), whole((slots, wide)), whole((slots, wide))],
        out_specs=pl.BlockSpec((row_block, wide), lambda i: (i, 0)),
        out_shape=jax.ShapeDtypeStruct((n_left, wide), f32),
        compiler_params=pltpu.CompilerParams(vmem_limit_bytes=48 << 20),
        name="left_sum",
    )(group_arg, ids, d_hi, d_lo)

    group_block = lambda lanes: pl.BlockSpec((edges, lanes), lambda i: (i, 0))
    grad_right = pl.pallas_call(
        right_kernel,
        grid=(groups,),
        in_specs=[group_block(wide), group_block(n_right), group_block(n_right)],
        out_specs=whole((n_right, wide)),
        out_shape=jax.ShapeDtypeStruct((n_right, wide), f32),
        scratch_shapes=[pltpu.VMEM((wide, n_right), f32)],
        compiler_params=pltpu.CompilerParams(vmem_limit_bytes=48 << 20),
        cost_estimate=pl.CostEstimate(flops=4 * slots * wide * n_right, bytes_accessed=6 * slots * wide, transcendentals=0),
        name="right_sum",
    )(query, c_hi, c_lo)

    for bit in bits_of(n_col):
        grad_rel = grad_rel + swap(grad_rel, "col", n_col, bit)
    for bit in bits_of(n_row):
        grad_rel = grad_rel + swap(grad_rel, "row", n_row, bit)
    grad_left = reduce_chunks(grad_left, "col", n_col)
    grad_right = reduce_chunks(grad_right, "row", n_row)

    def adagrad(embedding, accumulator, gradient):
        new_accum = accumulator + jnp.sum(gradient * gradient, axis=-1) / width
        gradient = from_halves(gradient, width)
        return embedding - learn_rate * gradient / (jnp.sqrt(new_accum)[..., None] + epsilon), new_accum

    new_left, new_left_state = adagrad(left_emb[0], left_state[0], grad_left)
    new_right, new_right_state = adagrad(right_emb[0], right_state[0], grad_right)
    new_rel, new_rel_state = adagrad(relation, rel_state, grad_rel)
    return new_left[None], new_left_state[None], new_right[None], new_right_state[None], new_rel, new_rel_state


def solution(mesh):
    entities = (P("row", "col", None), P("row", "col"), P("col", "row", None), P("col", "row"), P(), P())
    return jax.shard_map(
        functools.partial(body, mesh.shape["row"], mesh.shape["col"]),
        mesh=mesh,
        in_specs=entities + (P("row", "col", None),) * 3 + (P("row", "col", None, None), P("row", "col")),
        out_specs=entities,
        check_vma=False,
    )
```

```python
import functools

import jax
import jax.numpy as jnp
from jax import lax
from jax.experimental import pallas as pl
from jax.experimental.pallas import tpu as pltpu
from jax.sharding import PartitionSpec as P

CH = 1000
LANES = 128
TILE = 512

learn_rate = 0.1
epsilon = 1e-10
bf16 = jnp.bfloat16
f32 = jnp.float32


def round_up(value, step):
    return (value + step - 1) // step * step


def to_halves(array, half_pad):
    half = array.shape[-1] // 2
    pad = [(0, 0)] * (array.ndim - 1) + [(0, half_pad - half)]
    return jnp.concatenate([jnp.pad(array[..., :half], pad), jnp.pad(array[..., half:], pad)], axis=-1)


def from_halves(array, width):
    half_pad = array.shape[-1] // 2
    return jnp.concatenate([array[..., : width // 2], array[..., half_pad : half_pad + width // 2]], axis=-1)


def bits_of(size):
    return [1 << b for b in range(size.bit_length() - 1)]


def swap(array, axis, size, bit):
    return lax.ppermute(array, axis, [(i, i ^ bit) for i in range(size)])


def tie(*arrays):
    return lax.optimization_barrier(arrays)


def gather_chunks(array, axis, size):
    for bit in reversed(bits_of(size)):
        array = jnp.concatenate([array, swap(array, axis, size, bit)], axis=0)
    return array


def reduce_chunks(array, axis, size):
    for bit in bits_of(size):
        half = array.shape[0] // 2
        array = array[:half] + swap(array[half:], axis, size, bit)
    return array


def routes(size):
    rest = bits_of(size)[1:]
    turn = len(rest) // 2
    return rest, rest[turn:] + rest[:turn]


def relative_ids(ids, axis, size, share):
    owner = ids // share
    within = ids - owner * share
    apart = owner ^ lax.axis_index(axis)
    place = jnp.zeros_like(apart)
    for s, bit in enumerate(reversed(bits_of(size))):
        place = place | jnp.where((apart & bit) != 0, 1 << s, 0)
    return place * share + within


def left_places(ids, size, share):
    owner = ids // share
    within = ids - owner * share
    apart = owner ^ lax.axis_index("col")
    half = share // 2
    quarter = size // 2 * half
    places = []
    for route in routes(size):
        place = jnp.zeros_like(apart)
        for s, bit in enumerate(reversed(route)):
            place = place | jnp.where((apart & bit) != 0, 1 << s, 0)
        places.append(place * half)
    first, second = places[0] + within, places[1] + within + (quarter - half)
    return (apart & 1) * (2 * quarter) + jnp.where(within < half, first, second)


def split_two(value):
    high = value.astype(bf16)
    return high, (value - high.astype(f32)).astype(bf16)


def dot(a, b):
    return jnp.dot(a, b, preferred_element_type=f32)


def edge_kernel(
    count_ref, ids_ref, mult_ref, left_ref, right_ref, rel_ref,
    query_ref, c_hi_ref, c_lo_ref, d_hi_ref, d_lo_ref, grad_rel_ref,
    rel_parts, right_t,
):
    step = pl.program_id(0)
    tile = ids_ref.shape[2]
    tiles_in_group = pl.num_programs(0) // mult_ref.shape[0]
    n_rel, wide = rel_ref.shape
    half = wide // 2
    n_left, n_right = left_ref.shape[0], right_ref.shape[0]
    rel_rows = rel_parts.shape[0]

    @pl.when(step == 0)
    def _():
        grad_rel_ref[...] = jnp.zeros_like(grad_rel_ref)
        rel_parts[...] = jnp.zeros_like(rel_parts)
        rest = rel_ref[...]
        for part in range(3):
            piece = rest.astype(bf16)
            rel_parts[part * n_rel : (part + 1) * n_rel, :] = piece
            rest = rest - piece.astype(f32)
        right_t[...] = right_ref[...].T

    group = step // tiles_in_group
    start = group * CH + (step - group * tiles_in_group) * tile

    @pl.when(start >= count_ref[0])
    def _():
        for ref in (query_ref, c_hi_ref, c_lo_ref, d_hi_ref, d_lo_ref):
            ref[...] = jnp.zeros_like(ref)

    @pl.when(start < count_ref[0])
    def _():
        ids = ids_ref[0]
        cols = ids.T
        left_col, rel_col, right_col = cols[:, 0:1], cols[:, 1:2], cols[:, 2:3]
        valid = cols[:, 3:4].astype(f32)
        rel_iota = lax.broadcasted_iota(jnp.int32, (tile, rel_rows), 1) % n_rel
        rel_hot = jnp.where(rel_iota == rel_col, 1.0, 0.0).astype(bf16)
        rel_vec = dot(rel_hot, rel_parts[...])
        left_iota = lax.broadcasted_iota(jnp.int32, (tile, n_left), 1)
        left_hot = jnp.where(left_iota == left_col, 1.0, 0.0).astype(bf16)
        left_vec = dot(left_hot, left_ref[...])
        a_re, a_im = left_vec[:, :half], left_vec[:, half:]
        b_re, b_im = rel_vec[:, :half], rel_vec[:, half:]
        query = jnp.concatenate([a_re * b_re - a_im * b_im, a_re * b_im + a_im * b_re], axis=1).astype(bf16)
        query_ref[...] = query
        scores = dot(query, right_t[...])
        mult = mult_ref[group]
        right_iota = lax.broadcasted_iota(jnp.int32, (tile, n_right), 1)
        is_target = right_iota == right_col
        positive = jnp.sum(jnp.where(is_target, scores, 0.0), axis=1, keepdims=True)
        masked = jnp.where(mult > 0.0, scores, -jnp.inf)
        highest = jnp.maximum(jnp.max(masked, axis=1, keepdims=True), positive)
        expo = jnp.exp(masked - highest)
        expo_pos = jnp.exp(positive - highest)
        totals = expo_pos + jnp.sum(expo * mult, axis=1, keepdims=True)
        probability = (expo * (valid / totals)).astype(bf16)
        pos_coeff = (expo_pos / totals - 1.0) * valid
        coeff = mult * probability.astype(f32) + jnp.where(is_target, pos_coeff, 0.0)
        c_hi, c_lo = split_two(coeff)
        c_hi_ref[...] = c_hi
        c_lo_ref[...] = c_lo
        d_query = dot(c_hi, right_ref[...]) + dot(c_lo, right_ref[...])
        g_re, g_im = d_query[:, :half], d_query[:, half:]
        d_left = jnp.concatenate([g_re * b_re + g_im * b_im, g_im * b_re - g_re * b_im], axis=1)
        d_hi, d_lo = split_two(d_left)
        d_hi_ref[...] = d_hi
        d_lo_ref[...] = d_lo
        d_rel = jnp.concatenate([g_re * a_re + g_im * a_im, g_im * a_re - g_re * a_im], axis=1)
        r_hi, r_lo = split_two(d_rel)
        row_iota = lax.broadcasted_iota(jnp.int32, (n_rel, tile), 0)
        rel_hot_t = jnp.where(row_iota == ids[1:2, :], 1.0, 0.0).astype(bf16)
        grad_rel_ref[...] += dot(rel_hot_t, r_hi) + dot(rel_hot_t, r_lo)


def left_kernel(base, groups_ref, ids_ref, d_hi_ref, d_lo_ref, out_ref):
    rows = out_ref.shape[0]
    edges = ids_ref.shape[2]
    out_ref[...] = jnp.zeros_like(out_ref)
    row_iota = lax.broadcasted_iota(jnp.int32, (rows, edges), 0) + (base + pl.program_id(0) * rows)

    def group_step(g, carry):
        hot = jnp.where(row_iota == ids_ref[g, 0:1, :], 1.0, 0.0).astype(bf16)
        here = pl.ds(pl.multiple_of(g * edges, edges), edges)
        out_ref[...] += dot(hot, d_hi_ref[here, :]) + dot(hot, d_lo_ref[here, :])
        return carry

    lax.fori_loop(0, groups_ref[0], group_step, 0)


def right_kernel(query_ref, c_hi_ref, c_lo_ref, out_ref, total):
    step = pl.program_id(0)

    @pl.when(step == 0)
    def _():
        total[...] = jnp.zeros_like(total)

    dims = (((0,), (0,)), ((), ()))
    query = query_ref[...]
    total[...] += lax.dot_general(query, c_hi_ref[...], dims, preferred_element_type=f32) + lax.dot_general(
        query, c_lo_ref[...], dims, preferred_element_type=f32
    )

    @pl.when(step == pl.num_programs(0) - 1)
    def _():
        out_ref[...] = total[...].T


def whole(shape):
    return pl.BlockSpec(shape, lambda *_: (0,) * len(shape))


def body(n_row, n_col, left_emb, left_state, right_emb, right_state, relation, rel_state, left_ids, rel_ids, right_ids, neg_ids, counts):
    width = relation.shape[1]
    half_pad = round_up(width // 2, LANES)
    wide = 2 * half_pad
    left_share, right_share = left_emb.shape[1], right_emb.shape[1]
    n_left, n_right, n_rel = left_share * n_col, right_share * n_row, relation.shape[0]
    groups = neg_ids.shape[2]
    edges = round_up(CH, TILE)
    slots = groups * edges
    tiles = edges // TILE

    edge_count = counts[0, 0]
    my_left = left_places(left_ids[0, 0], n_col, left_share).reshape(groups, CH)
    my_right = relative_ids(right_ids[0, 0], "row", n_row, right_share).reshape(groups, CH)
    my_neg = relative_ids(neg_ids[0, 0], "row", n_row, right_share)
    my_rel = rel_ids[0, 0].reshape(groups, CH)
    valid = (jnp.arange(groups * CH, dtype=jnp.int32) < edge_count).astype(jnp.int32).reshape(groups, CH)
    ids = jnp.stack([my_left, my_rel, my_right, valid] + [jnp.zeros_like(valid)] * 4, axis=1)
    ids = jnp.pad(ids, ((0, 0), (0, 0), (0, edges - CH)))
    hot = jnp.arange(n_right, dtype=jnp.int32)[None, :, None] == my_neg[:, None, :]
    mult = jnp.sum(hot.astype(f32), axis=2)[:, None, :]
    count_arg = edge_count.reshape(1)
    group_arg = (count_arg + CH - 1) // CH

    rel_wide = to_halves(relation, half_pad)
    right_mine = to_halves(right_emb[0].astype(bf16), half_pad)
    mine = to_halves(left_emb[0].astype(bf16), half_pad)
    part_a, part_b = mine[: left_share // 2], mine[left_share // 2 :]
    route_a, route_b = routes(n_col)
    right_part = gather_chunks(right_mine, "row", n_row)
    for step, (bit_a, bit_b) in enumerate(zip(reversed(route_a), reversed(route_b))):
        part_a, part_b = tie(part_a, part_b)
        more_a, more_b = tie(swap(part_a, "col", n_col, bit_a), swap(part_b, "col", n_col, bit_b))
        part_a = jnp.concatenate([part_a, more_a], axis=0)
        part_b = jnp.concatenate([part_b, more_b], axis=0)
    own = jnp.concatenate([part_a, part_b], axis=0)
    own, ids, mult, right_part, rel_wide, count_arg, group_arg = tie(own, ids, mult, right_part, rel_wide, count_arg, group_arg)
    left_part = jnp.concatenate([own, swap(own, "col", n_col, 1)], axis=0)

    smem = pl.BlockSpec(memory_space=pltpu.SMEM)
    tile_block = lambda lanes: pl.BlockSpec((TILE, lanes), lambda i: (i, 0))
    query, c_hi, c_lo, d_hi, d_lo, grad_rel = pl.pallas_call(
        edge_kernel,
        grid=(groups * tiles,),
        in_specs=[
            smem,
            pl.BlockSpec((1, 8, TILE), lambda i: (i // tiles, 0, i % tiles)),
            whole((groups, 1, n_right)),
            whole((n_left, wide)),
            whole((n_right, wide)),
            whole((n_rel, wide)),
        ],
        out_specs=[
            tile_block(wide),
            tile_block(n_right),
            tile_block(n_right),
            tile_block(wide),
            tile_block(wide),
            whole((n_rel, wide)),
        ],
        out_shape=[
            jax.ShapeDtypeStruct((slots, wide), bf16),
            jax.ShapeDtypeStruct((slots, n_right), bf16),
            jax.ShapeDtypeStruct((slots, n_right), bf16),
            jax.ShapeDtypeStruct((slots, wide), bf16),
            jax.ShapeDtypeStruct((slots, wide), bf16),
            jax.ShapeDtypeStruct((n_rel, wide), f32),
        ],
        scratch_shapes=[
            pltpu.VMEM((round_up(3 * n_rel, LANES), wide), bf16),
            pltpu.VMEM((wide, n_right), bf16),
        ],
        compiler_params=pltpu.CompilerParams(vmem_limit_bytes=48 << 20),
        name="edges",
    )(count_arg, ids, mult, left_part, right_part, rel_wide)

    piece = n_left // 4
    row_block = min(piece, left_share * 4)

    def left_sum(quarter, d_hi, d_lo):
        return pl.pallas_call(
            functools.partial(left_kernel, quarter * piece),
            grid=(piece // row_block,),
            in_specs=[smem, whole((groups, 8, edges)), whole((slots, wide)), whole((slots, wide))],
            out_specs=pl.BlockSpec((row_block, wide), lambda i: (i, 0)),
            out_shape=jax.ShapeDtypeStruct((piece, wide), f32),
            compiler_params=pltpu.CompilerParams(vmem_limit_bytes=48 << 20),
            cost_estimate=pl.CostEstimate(flops=4 * slots * wide * piece, bytes_accessed=4 * slots * wide, transcendentals=0),
            name="left_sum",
        )(group_arg, ids, d_hi, d_lo)

    def right_sum(query, c_hi, c_lo):
        group_block = lambda lanes: pl.BlockSpec((edges, lanes), lambda i: (i, 0))
        return pl.pallas_call(
            right_kernel,
            grid=(groups,),
            in_specs=[group_block(wide), group_block(n_right), group_block(n_right)],
            out_specs=whole((n_right, wide)),
            out_shape=jax.ShapeDtypeStruct((n_right, wide), f32),
            scratch_shapes=[pltpu.VMEM((wide, n_right), f32)],
            compiler_params=pltpu.CompilerParams(vmem_limit_bytes=48 << 20),
            cost_estimate=pl.CostEstimate(flops=4 * slots * wide * n_right, bytes_accessed=6 * slots * wide, transcendentals=0),
            name="right_sum",
        )(query, c_hi, c_lo)

    rel_steps = [("col", n_col, bit) for bit in bits_of(n_col)] + [("row", n_row, bit) for bit in bits_of(n_row)]

    def add_rel(total, last=False):
        for _ in range(len(rel_steps) if last else 1):
            if rel_steps:
                total = total + swap(total, *rel_steps.pop(0))
        return total

    far_a, next_rel = left_sum(2, d_hi, d_lo), add_rel(grad_rel)
    far_a, grad_rel, d_hi, d_lo = tie(far_a, next_rel, d_hi, d_lo)
    far_b, next_rel = left_sum(3, d_hi, d_lo), add_rel(grad_rel)
    far_a, far_b, grad_rel, d_hi, d_lo = tie(far_a, far_b, next_rel, d_hi, d_lo)
    come_a = swap(far_a, "col", n_col, 1)
    near_a, next_rel = left_sum(0, d_hi, d_lo), add_rel(grad_rel)
    near_a, come_a, grad_rel, far_b, d_hi, d_lo = tie(near_a, come_a, next_rel, far_b, d_hi, d_lo)
    come_b = swap(far_b, "col", n_col, 1)
    near_b, next_rel = left_sum(1, d_hi, d_lo), add_rel(grad_rel)
    near_b, come_b, grad_rel, query, c_hi, c_lo = tie(near_b, come_b, next_rel, query, c_hi, c_lo)
    sum_a, sum_b = tie(near_a + come_a, near_b + come_b)
    grad_right = None
    for bit_a, bit_b in zip(route_a, route_b):
        half = sum_a.shape[0] // 2
        more_a, more_b = swap(sum_a[half:], "col", n_col, bit_a), swap(sum_b[half:], "col", n_col, bit_b)
        if grad_right is None:
            grad_right, next_rel = right_sum(query, c_hi, c_lo), add_rel(grad_rel, last=True)
            more_a, more_b, grad_right, grad_rel = tie(more_a, more_b, grad_right, next_rel)
        else:
            more_a, more_b = tie(more_a, more_b)
        sum_a, sum_b = tie(sum_a[:half] + more_a, sum_b[:half] + more_b)
    grad_left = jnp.concatenate([sum_a, sum_b], axis=0)
    grad_right = reduce_chunks(grad_right, "row", n_row)

    def adagrad(embedding, accumulator, gradient):
        new_accum = accumulator + jnp.sum(gradient * gradient, axis=-1) / width
        gradient = from_halves(gradient, width)
        return embedding - learn_rate * gradient / (jnp.sqrt(new_accum)[..., None] + epsilon), new_accum

    new_left, new_left_state = adagrad(left_emb[0], left_state[0], grad_left)
    new_right, new_right_state = adagrad(right_emb[0], right_state[0], grad_right)
    new_rel, new_rel_state = adagrad(relation, rel_state, grad_rel)
    return new_left[None], new_left_state[None], new_right[None], new_right_state[None], new_rel, new_rel_state


def solution(mesh):
    entities = (P("row", "col", None), P("row", "col"), P("col", "row", None), P("col", "row"), P(), P())
    return jax.shard_map(
        functools.partial(body, mesh.shape["row"], mesh.shape["col"]),
        mesh=mesh,
        in_specs=entities + (P("row", "col", None),) * 3 + (P("row", "col", None, None), P("row", "col")),
        out_specs=entities,
        check_vma=False,
    )
```

```python
import functools

import jax
import jax.numpy as jnp
from jax import lax
from jax.experimental import pallas as pl
from jax.experimental.pallas import tpu as pltpu
from jax.sharding import PartitionSpec as P

CH = 1000
LANES = 128
TILE = 1024
SUB = 512
WINDOW = 128
SPAN = 512

learn_rate = 0.1
epsilon = 1e-10
bf16 = jnp.bfloat16
f32 = jnp.float32


def round_up(value, step):
    return (value + step - 1) // step * step


def to_halves(array, half_pad):
    half = array.shape[-1] // 2
    pad = [(0, 0)] * (array.ndim - 1) + [(0, half_pad - half)]
    return jnp.concatenate([jnp.pad(array[..., :half], pad), jnp.pad(array[..., half:], pad)], axis=-1)


def from_halves(array, width):
    half_pad = array.shape[-1] // 2
    return jnp.concatenate([array[..., : width // 2], array[..., half_pad : half_pad + width // 2]], axis=-1)


def bits_of(size):
    return [1 << b for b in range(size.bit_length() - 1)]


def swap(array, axis, size, bit):
    return lax.ppermute(array, axis, [(i, i ^ bit) for i in range(size)])


def tie(*arrays):
    return lax.optimization_barrier(arrays)


def gather_chunks(array, axis, size):
    for bit in reversed(bits_of(size)):
        array = jnp.concatenate([array, swap(array, axis, size, bit)], axis=0)
    return array


def reduce_chunks(array, axis, size):
    for bit in bits_of(size):
        half = array.shape[0] // 2
        array = array[:half] + swap(array[half:], axis, size, bit)
    return array


def routes(size):
    rest = bits_of(size)[1:]
    turn = len(rest) // 2
    return rest, rest[turn:] + rest[:turn]


def spread(apart, route):
    place = jnp.zeros_like(apart)
    for s, bit in enumerate(reversed(route)):
        place = place | jnp.where((apart & bit) != 0, 1 << s, 0)
    return place


def owner_of(ids, share):
    owner = ((ids.astype(f32) + 0.5) * (1.0 / share)).astype(jnp.int32)
    return owner, ids - owner * share


def right_places(ids, me, size, share):
    owner, within = owner_of(ids, share)
    return spread(owner ^ me, bits_of(size)) * share + within


def left_places(ids, me, size, share):
    owner, within = owner_of(ids, share)
    apart = owner ^ me
    half = share // 2
    quarter = size // 2 * half
    first, second = (spread(apart, route) * half for route in routes(size))
    return (apart & 1) * (2 * quarter) + jnp.where(within < half, first + within, second + within + (quarter - half))


def prep_kernel(n_row, n_col, left_share, rows, where_ref, raw_ref, ids_ref, mult_ref, bound_ref):
    groups, _, edges = raw_ref.shape
    n_right = mult_ref.shape[2]
    n_left = left_share * n_col
    count, me_col, me_row = where_ref[0], where_ref[1], where_ref[2]

    def group_step(g, carry):
        raw = raw_ref[g]
        slot = lax.broadcasted_iota(jnp.int32, (1, edges), 1)
        real = slot < CH
        valid = real & (slot + g * CH < count)
        left = jnp.where(valid, left_places(raw[0:1], me_col, n_col, left_share), n_left)
        right = right_places(raw[2:3], me_row, n_row, n_right // n_row)
        neg = jnp.where(real, right_places(raw[3:4], me_row, n_row, n_right // n_row), -1)
        key = left * edges + slot
        rows_in = [key, neg, left >> 6, left & 63, raw[1:2], right >> 6, right & 63, valid.astype(jnp.int32)]
        cols = jnp.concatenate(rows_in, axis=0).T
        payload = cols.astype(f32).astype(bf16)
        rank = jnp.zeros((8, edges), jnp.int32)
        mult = jnp.zeros((8, n_right), f32)
        bound = jnp.zeros((8, LANES), jnp.int32)
        lane_start = lax.broadcasted_iota(jnp.int32, (LANES, LANES), 1) * rows
        lane_right = lax.broadcasted_iota(jnp.int32, (LANES, n_right), 1)
        for k in range(edges // LANES):
            part = cols[k * LANES : (k + 1) * LANES]
            less = jnp.where(part[:, 0:1] < key, 1, 0)
            rank = rank + jnp.sum(less.reshape(LANES // 8, 8, edges), axis=0)
            same = jnp.where(part[:, 1:2] == lane_right, 1.0, 0.0)
            mult = mult + jnp.sum(same.reshape(LANES // 8, 8, n_right), axis=0)
            below = jnp.where(part[:, 2:3] * 64 + part[:, 3:4] < lane_start, 1, 0)
            bound = bound + jnp.sum(below.reshape(LANES // 8, 8, LANES), axis=0)
        rank = jnp.sum(rank, axis=0, keepdims=True)
        mult_ref[g] = jnp.sum(mult, axis=0, keepdims=True)
        bound_ref[g] = jnp.sum(bound, axis=0, keepdims=True)
        moved = []
        for k in range(edges // LANES):
            place = lax.broadcasted_iota(jnp.int32, (LANES, edges), 0) + k * LANES
            moved.append(dot(jnp.where(place == rank, 1.0, 0.0).astype(bf16), payload))
        moved = jnp.concatenate(moved, axis=0).T.astype(jnp.int32)
        out = [moved[2:3] * 64 + moved[3:4], moved[4:5], moved[5:6] * 64 + moved[6:7], moved[7:8]]
        ids_ref[g] = jnp.concatenate(out + out, axis=0)
        return carry

    lax.fori_loop(0, groups, group_step, 0)


def split_two(value):
    high = value.astype(bf16)
    return high, (value - high.astype(f32)).astype(bf16)


def packed_rows(rows):
    return 3 * rows + 8


def pack(value, tail):
    rows = value.shape[0]
    lane = lax.broadcasted_iota(jnp.int32, (rows, LANES), 1)
    first, second, third, fourth = (value[:, k * LANES : (k + 1) * LANES] for k in range(4))
    mixed = jnp.where(lane < tail, second, pltpu.roll(fourth, tail, 1))
    spill = 2 * tail - LANES
    last = jnp.zeros((8, LANES), f32)
    for k in range(rows // 8):
        moved = pltpu.roll(fourth[8 * k : 8 * k + 8], (spill * k + tail) % LANES, 1)
        place = lane[:8] - spill * k
        last = jnp.where((place >= 0) & (place < spill), moved, last)
    return jnp.concatenate([first, third, mixed, last], axis=0)


def unpack(value, rows, tail):
    lane = lax.broadcasted_iota(jnp.int32, (rows, LANES), 1)
    first, third, mixed = (value[k * rows : (k + 1) * rows] for k in range(3))
    last = value[3 * rows :]
    spill = 2 * tail - LANES
    turned = pltpu.roll(third, tail, 1)
    fourth = [pltpu.roll(last, (LANES - spill * k) % LANES, 1) for k in range(rows // 8)]
    fourth = jnp.where(lane < spill, jnp.concatenate(fourth, axis=0), 0.0)
    return first, jnp.where(lane < tail, mixed, turned), jnp.where(lane < tail, turned, mixed), fourth


def finish_kernel(parts, chunk, tail, *refs):
    n_grads = sum(len(p) for p in parts)
    grads, (emb_ref, state_ref, new_ref, new_state_ref) = refs[:n_grads], refs[n_grads:]
    width = emb_ref.shape[1]
    means, tiles_of = [], []
    for part in parts:
        total = grads[part[0]][...]
        for k in part[1:]:
            total = total + grads[k][...]
        size = packed_rows(chunk)
        for k in range(total.shape[0] // size):
            tiles = unpack(total[k * size : (k + 1) * size], chunk, tail)
            squares = sum(t * t for t in tiles)
            means.append(jnp.sum(squares, axis=1, keepdims=True) / width)
            tiles_of.append(tiles)
    rows = chunk * len(means)
    mean = jnp.broadcast_to(jnp.concatenate(means, axis=0), (rows, LANES))
    state = jnp.broadcast_to(state_ref[...], (LANES, rows)).T
    accum = state + mean
    new_state_ref[...] = accum.T[0:1, :]
    rate = learn_rate / (jnp.sqrt(accum) + epsilon)
    for k, tiles in enumerate(tiles_of):
        here = slice(k * chunk, (k + 1) * chunk)
        for j, tile in enumerate(tiles):
            low, high = j * LANES, min((j + 1) * LANES, width)
            new_ref[here, low:high] = emb_ref[here, low:high] - (rate[here] * tile)[:, : high - low]


def finish(parts, chunk, tail, grads, embedding, state, name):
    return pl.pallas_call(
        functools.partial(finish_kernel, parts, chunk, tail),
        out_shape=[jax.ShapeDtypeStruct(embedding.shape, f32), jax.ShapeDtypeStruct((1, embedding.shape[0]), f32)],
        name=name,
    )(*grads, embedding, state.reshape(1, -1))


def dot(a, b):
    return jnp.dot(a, b, preferred_element_type=f32)


def edge_kernel(
    rows, chunk, tail, count_ref, bound_ref, ids_ref, mult_ref, left_ref, right_ref, rel_ref,
    query_ref, c_hi_ref, c_lo_ref, rel_out_ref, near_ref, far_ref,
    rel_parts, right_t, d_hi_ref, d_lo_ref, grad_rel_ref, piece_ref,
):
    step = pl.program_id(0)
    tile = query_ref.shape[0]
    groups, _, edges = ids_ref.shape
    tiles_in_group = pl.num_programs(0) // mult_ref.shape[0]
    n_rel, wide = rel_ref.shape
    half = wide // 2
    n_left, n_right = left_ref.shape[0], right_ref.shape[0]
    rel_rows = rel_parts.shape[0]

    @pl.when(step == 0)
    def _():
        grad_rel_ref[...] = jnp.zeros_like(grad_rel_ref)
        rel_parts[...] = jnp.zeros_like(rel_parts)
        rest = rel_ref[...]
        for part in range(3):
            piece = rest.astype(bf16)
            rel_parts[part * n_rel : (part + 1) * n_rel, :] = piece
            rest = rest - piece.astype(f32)
        right_t[...] = right_ref[...].T

    group = step // tiles_in_group
    start = group * CH + (step - group * tiles_in_group) * tile

    @pl.when(start >= count_ref[0])
    def _():
        for ref in (query_ref, c_hi_ref, c_lo_ref):
            ref[...] = jnp.zeros_like(ref)
        here = pl.ds(pl.multiple_of(step * tile, tile), tile)
        d_hi_ref[here, :] = jnp.zeros((tile, wide), bf16)
        d_lo_ref[here, :] = jnp.zeros((tile, wide), bf16)

    @pl.when(start < count_ref[0])
    def _():
        place = pl.multiple_of((step - group * tiles_in_group) * tile, tile)
        ids = ids_ref[group, :, pl.ds(place, tile)]
        all_cols = ids.T
        mult = mult_ref[group]
        absent = jnp.where(mult > 0.0, 0.0, -jnp.inf)

        def fetch(sub):
            cols = all_cols[sub * SUB : (sub + 1) * SUB]
            left_col, rel_col = cols[:, 0:1], cols[:, 1:2]
            rel_iota = lax.broadcasted_iota(jnp.int32, (SUB, rel_rows), 1) % n_rel
            rel_hot = jnp.where(rel_iota == rel_col, 1.0, 0.0).astype(bf16)
            rel_vec = dot(rel_hot, rel_parts[...])
            left_iota = lax.broadcasted_iota(jnp.int32, (SUB, n_left), 1)
            left_hot = jnp.where(left_iota == left_col, 1.0, 0.0).astype(bf16)
            left_vec = dot(left_hot, left_ref[...])
            a_re, a_im = left_vec[:, :half], left_vec[:, half:]
            b_re, b_im = rel_vec[:, :half], rel_vec[:, half:]
            query = jnp.concatenate([a_re * b_re - a_im * b_im, a_re * b_im + a_im * b_re], axis=1).astype(bf16)
            query_ref[sub * SUB : (sub + 1) * SUB, :] = query
            return (a_re, a_im, b_re, b_im), dot(query, right_t[...])

        def weigh(sub, scores):
            cols = all_cols[sub * SUB : (sub + 1) * SUB]
            right_col, valid = cols[:, 2:3], cols[:, 3:4].astype(f32)
            right_iota = lax.broadcasted_iota(jnp.int32, (SUB, n_right), 1)
            is_target = right_iota == right_col
            positive = jnp.sum(jnp.where(is_target, scores, 0.0), axis=1, keepdims=True)
            masked = scores + absent
            highest = jnp.maximum(jnp.max(masked, axis=1, keepdims=True), positive)
            expo = jnp.exp(masked - highest)
            expo_pos = jnp.exp(positive - highest)
            totals = expo_pos + jnp.sum(expo * mult, axis=1, keepdims=True)
            probability = (expo * (valid / totals)).astype(bf16)
            pos_coeff = (expo_pos / totals - 1.0) * valid
            coeff = mult * probability.astype(f32) + jnp.where(is_target, pos_coeff, 0.0)
            c_hi, c_lo = split_two(coeff)
            c_hi_ref[sub * SUB : (sub + 1) * SUB, :] = c_hi
            c_lo_ref[sub * SUB : (sub + 1) * SUB, :] = c_lo
            return c_hi, c_lo

        def back(sub, parts, coeffs):
            a_re, a_im, b_re, b_im = parts
            d_query = dot(coeffs[0], right_ref[...]) + dot(coeffs[1], right_ref[...])
            g_re, g_im = d_query[:, :half], d_query[:, half:]
            d_left = jnp.concatenate([g_re * b_re + g_im * b_im, g_im * b_re - g_re * b_im], axis=1)
            d_hi, d_lo = split_two(d_left)
            here = pl.ds(pl.multiple_of(step * tile + sub * SUB, SUB), SUB)
            d_hi_ref[here, :] = d_hi
            d_lo_ref[here, :] = d_lo
            d_rel = jnp.concatenate([g_re * a_re + g_im * a_im, g_im * a_re - g_re * a_im], axis=1)
            r_hi, r_lo = split_two(d_rel)
            row_iota = lax.broadcasted_iota(jnp.int32, (n_rel, SUB), 0)
            rel_hot_t = jnp.where(row_iota == ids[1:2, sub * SUB : (sub + 1) * SUB], 1.0, 0.0).astype(bf16)
            return dot(rel_hot_t, r_hi) + dot(rel_hot_t, r_lo)

        subs = tile // SUB
        fetched, weighed, rel_total = {}, {}, 0.0
        for turn in range(subs + 2):
            if turn < subs:
                fetched[turn] = fetch(turn)
            if 0 <= turn - 1 < subs:
                weighed[turn - 1] = weigh(turn - 1, fetched[turn - 1][1])
            if 0 <= turn - 2 < subs:
                rel_total += back(turn - 2, fetched[turn - 2][0], weighed[turn - 2])
        grad_rel_ref[...] += rel_total

    @pl.when(step == pl.num_programs(0) - 1)
    def _():
        n_pieces = n_left // rows

        def hot_rows(g, base, at, size):
            row_iota = lax.broadcasted_iota(jnp.int32, (rows, size), 0) + base
            return jnp.where(row_iota == ids_ref[g, 0:1, pl.ds(at, size)], 1.0, 0.0).astype(bf16)

        def span(g, piece):
            return jnp.minimum(bound_ref[g, piece] // WINDOW * WINDOW, edges - SPAN)

        few = n_rel // 2
        for k in range(2):
            size = packed_rows(few)
            rel_out_ref[k * size : (k + 1) * size, :] = pack(grad_rel_ref[k * few : (k + 1) * few, :], tail)

        def piece_step(piece, out_ref, shift):
            base = pl.multiple_of(piece * rows, rows)
            total = jnp.zeros((rows, wide), f32)
            for g in range(groups):
                at = pl.multiple_of(span(g, piece), WINDOW)
                hot = hot_rows(g, base, at, SPAN)
                here = pl.ds(pl.multiple_of(g * edges + at, WINDOW), SPAN)
                total = total + dot(hot, d_hi_ref[here, :]) + dot(hot, d_lo_ref[here, :])
            piece_ref[...] = total

            def rest_step(g, carry):
                def window_step(w, inner):
                    at = pl.multiple_of(w * WINDOW, WINDOW)
                    hot = hot_rows(g, base, at, WINDOW)
                    here = pl.ds(pl.multiple_of(g * edges + at, WINDOW), WINDOW)
                    piece_ref[...] += dot(hot, d_hi_ref[here, :]) + dot(hot, d_lo_ref[here, :])
                    return inner

                first = (span(g, piece) + SPAN) // WINDOW
                return lax.fori_loop(first, (bound_ref[g, piece + 1] + WINDOW - 1) // WINDOW, window_step, carry)

            lax.fori_loop(0, groups, rest_step, 0)
            size = packed_rows(chunk)
            for k in range(rows // chunk):
                there = pl.ds(pl.multiple_of((piece - shift) * (rows // chunk) * size + k * size, 8), size)
                out_ref[there, :] = pack(piece_ref[k * chunk : (k + 1) * chunk, :], tail)

        for shift, out_ref in ((0, near_ref), (n_pieces // 2, far_ref)):

            def each(k, carry, shift=shift, out_ref=out_ref):
                piece_step(k + shift, out_ref, shift)
                return carry

            lax.fori_loop(0, n_pieces // 2, each, 0)


def right_kernel(query_ref, c_hi_ref, c_lo_ref, out_ref, total):
    step = pl.program_id(0)

    @pl.when(step == 0)
    def _():
        total[...] = jnp.zeros_like(total)

    dims = (((0,), (0,)), ((), ()))
    query = query_ref[...]
    total[...] += lax.dot_general(query, c_hi_ref[...], dims, preferred_element_type=f32) + lax.dot_general(
        query, c_lo_ref[...], dims, preferred_element_type=f32
    )

    @pl.when(step == pl.num_programs(0) - 1)
    def _():
        out_ref[...] = total[...].T


def whole(shape):
    return pl.BlockSpec(shape, lambda *_: (0,) * len(shape))


def body(n_row, n_col, left_emb, left_state, right_emb, right_state, relation, rel_state, left_ids, rel_ids, right_ids, neg_ids, counts):
    width = relation.shape[1]
    half_pad = round_up(width // 2, LANES)
    wide = 2 * half_pad
    left_share, right_share = left_emb.shape[1], right_emb.shape[1]
    n_left, n_right, n_rel = left_share * n_col, right_share * n_row, relation.shape[0]
    groups = neg_ids.shape[2]
    edges = round_up(CH, TILE)
    slots = groups * edges
    tile = TILE if n_right <= SUB else SUB
    tiles = edges // tile

    smem = pl.BlockSpec(memory_space=pltpu.SMEM)
    rows = left_share * 4
    count_arg = counts.reshape(1)
    where = jnp.stack([counts[0, 0], lax.axis_index("col"), lax.axis_index("row")])
    raw = jnp.stack([a.reshape(groups, CH) for a in (left_ids, rel_ids, right_ids, neg_ids)], axis=1)
    raw = jnp.pad(raw, ((0, 0), (0, 0), (0, edges - CH)))
    ids, mult, bound = pl.pallas_call(
        functools.partial(prep_kernel, n_row, n_col, left_share, rows),
        in_specs=[smem, whole((groups, 4, edges))],
        out_specs=[whole((groups, 8, edges)), whole((groups, 1, n_right)), whole((groups, 1, LANES))],
        out_shape=[
            jax.ShapeDtypeStruct((groups, 8, edges), jnp.int32),
            jax.ShapeDtypeStruct((groups, 1, n_right), f32),
            jax.ShapeDtypeStruct((groups, 1, LANES), jnp.int32),
        ],
        cost_estimate=pl.CostEstimate(flops=16 * slots * edges, bytes_accessed=32 * slots, transcendentals=0),
        compiler_params=pltpu.CompilerParams(vmem_limit_bytes=32 << 20),
        name="prep",
    )(where, raw)
    bound = bound.reshape(groups, LANES)

    rel_wide = to_halves(relation, half_pad)
    right_mine = to_halves(right_emb[0].astype(bf16), half_pad)
    mine = to_halves(left_emb[0].astype(bf16), half_pad)
    part_a, part_b = mine[: left_share // 2], mine[left_share // 2 :]
    route_a, route_b = routes(n_col)
    right_part = gather_chunks(right_mine, "row", n_row)
    for step, (bit_a, bit_b) in enumerate(zip(reversed(route_a), reversed(route_b))):
        part_a, part_b = tie(part_a, part_b)
        more_a, more_b = tie(swap(part_a, "col", n_col, bit_a), swap(part_b, "col", n_col, bit_b))
        part_a = jnp.concatenate([part_a, more_a], axis=0)
        part_b = jnp.concatenate([part_b, more_b], axis=0)
    own = jnp.concatenate([part_a, part_b], axis=0)
    own, ids, mult, bound, right_part, rel_wide = tie(own, ids, mult, bound, right_part, rel_wide)
    left_part = jnp.concatenate([own, swap(own, "col", n_col, 1)], axis=0)

    tile_block = lambda lanes: pl.BlockSpec((tile, lanes), lambda i: (i, 0))
    chunk, tail = left_share // 2, width // 2 - LANES
    packed_half = n_left // 2 // chunk * packed_rows(chunk)
    packed_rel = 2 * packed_rows(n_rel // 2)
    query, c_hi, c_lo, grad_rel, near, far = pl.pallas_call(
        functools.partial(edge_kernel, rows, chunk, tail),
        grid=(groups * tiles,),
        in_specs=[
            smem,
            smem,
            whole((groups, 8, edges)),
            whole((groups, 1, n_right)),
            whole((n_left, wide)),
            whole((n_right, wide)),
            whole((n_rel, wide)),
        ],
        out_specs=[
            tile_block(wide),
            tile_block(n_right),
            tile_block(n_right),
            whole((packed_rel, LANES)),
            whole((packed_half, LANES)),
            whole((packed_half, LANES)),
        ],
        out_shape=[
            jax.ShapeDtypeStruct((slots, wide), bf16),
            jax.ShapeDtypeStruct((slots, n_right), bf16),
            jax.ShapeDtypeStruct((slots, n_right), bf16),
            jax.ShapeDtypeStruct((packed_rel, LANES), f32),
            jax.ShapeDtypeStruct((packed_half, LANES), f32),
            jax.ShapeDtypeStruct((packed_half, LANES), f32),
        ],
        scratch_shapes=[
            pltpu.VMEM((round_up(3 * n_rel, LANES), wide), bf16),
            pltpu.VMEM((wide, n_right), bf16),
            pltpu.VMEM((slots, wide), bf16),
            pltpu.VMEM((slots, wide), bf16),
            pltpu.VMEM((n_rel, wide), f32),
            pltpu.VMEM((rows, wide), f32),
        ],
        compiler_params=pltpu.CompilerParams(vmem_limit_bytes=56 << 20),
        name="edges",
    )(count_arg, bound, ids, mult, left_part, right_part, rel_wide)

    def right_sum(query, c_hi, c_lo):
        group_block = lambda lanes: pl.BlockSpec((edges, lanes), lambda i: (i, 0))
        return pl.pallas_call(
            right_kernel,
            grid=(groups,),
            in_specs=[group_block(wide), group_block(n_right), group_block(n_right)],
            out_specs=whole((n_right, wide)),
            out_shape=jax.ShapeDtypeStruct((n_right, wide), f32),
            scratch_shapes=[pltpu.VMEM((wide, n_right), f32)],
            compiler_params=pltpu.CompilerParams(vmem_limit_bytes=48 << 20),
            cost_estimate=pl.CostEstimate(flops=4 * slots * wide * n_right, bytes_accessed=6 * slots * wide, transcendentals=0),
            name="right_sum",
        )(query, c_hi, c_lo)

    odd = lax.rem(lax.axis_index("col"), 2) == 1
    few = packed_rel // 2
    grad_rel = jnp.where(odd, grad_rel[few:], grad_rel[:few]) + swap(
        jnp.where(odd, grad_rel[:few], grad_rel[few:]), "col", n_col, 1
    )
    for bit in bits_of(n_row):
        grad_rel = grad_rel + swap(grad_rel, "row", n_row, bit)
    come, grad_rel = tie(swap(far, "col", n_col, 1), grad_rel)
    half = packed_half // 2
    sum_a = jnp.concatenate([near[:half] + come[:half], grad_rel], axis=0)
    sum_b = near[half:] + come[half:]
    sum_a, sum_b, query, c_hi, c_lo = tie(sum_a, sum_b, query, c_hi, c_lo)
    grad_right = None
    for bit_a, bit_b in zip(route_a, route_b):
        half = sum_b.shape[0] // 2
        more_a, more_b = swap(sum_a[half:], "col", n_col, bit_a), swap(sum_b[half:], "col", n_col, bit_b)
        if grad_right is None:
            grad_right = right_sum(query, c_hi, c_lo)
            more_a, more_b, grad_right = tie(more_a, more_b, grad_right)
        else:
            more_a, more_b = tie(more_a, more_b)
        keep_a, keep_b, keep_rel = sum_a[:half], sum_b[:half], sum_a[2 * half :]
        if half > packed_rows(chunk):
            sum_a = jnp.concatenate([keep_a + more_a[:half], keep_rel + more_a[half:]], axis=0)
            sum_a, sum_b = tie(sum_a, keep_b + more_b)
    grad_rel = keep_rel + more_a[half:]
    other = swap(grad_rel, "col", n_col, 1)
    new_left, new_left_state = finish(
        ((0, 1), (2, 3)), chunk, tail, (keep_a, more_a[:half], keep_b, more_b), left_emb[0], left_state, "new_left"
    )
    grad_rel = jnp.concatenate([jnp.where(odd, other, grad_rel), jnp.where(odd, grad_rel, other)], axis=0)
    new_rel, new_rel_state = finish(((0,),), n_rel // 2, tail, (grad_rel,), relation, rel_state, "new_rel")
    grad_right = reduce_chunks(grad_right, "row", n_row)

    def adagrad(embedding, accumulator, gradient):
        new_accum = accumulator + jnp.sum(gradient * gradient, axis=-1) / width
        gradient = from_halves(gradient, width)
        return embedding - learn_rate * gradient / (jnp.sqrt(new_accum)[..., None] + epsilon), new_accum

    new_right, new_right_state = adagrad(right_emb[0], right_state[0], grad_right)
    return new_left[None], new_left_state, new_right[None], new_right_state[None], new_rel, new_rel_state[0]


def solution(mesh):
    entities = (P("row", "col", None), P("row", "col"), P("col", "row", None), P("col", "row"), P(), P())
    return jax.shard_map(
        functools.partial(body, mesh.shape["row"], mesh.shape["col"]),
        mesh=mesh,
        in_specs=entities + (P("row", "col", None),) * 3 + (P("row", "col", None, None), P("row", "col")),
        out_specs=entities,
        check_vma=False,
    )
```

```python
import functools

import jax
import jax.numpy as jnp
from jax import lax
from jax.experimental import pallas as pl
from jax.experimental.pallas import tpu as pltpu
from jax.sharding import PartitionSpec as P

CH = 1000
LANES = 128
TILE = 1024
SUB = 512
WINDOW = 128
SPAN = 512
RIGHT_CHUNK = 64

learn_rate = 0.1
epsilon = 1e-10
bf16 = jnp.bfloat16
f32 = jnp.float32


def round_up(value, step):
    return (value + step - 1) // step * step


def to_halves(array, half_pad):
    half = array.shape[-1] // 2
    pad = [(0, 0)] * (array.ndim - 1) + [(0, half_pad - half)]
    return jnp.concatenate([jnp.pad(array[..., :half], pad), jnp.pad(array[..., half:], pad)], axis=-1)


def from_halves(array, width):
    half_pad = array.shape[-1] // 2
    return jnp.concatenate([array[..., : width // 2], array[..., half_pad : half_pad + width // 2]], axis=-1)


def bits_of(size):
    return [1 << b for b in range(size.bit_length() - 1)]


def swap(array, axis, size, bit):
    return lax.ppermute(array, axis, [(i, i ^ bit) for i in range(size)])


def tie(*arrays):
    return lax.optimization_barrier(arrays)


def gather_chunks(array, axis, size):
    for bit in reversed(bits_of(size)):
        array = jnp.concatenate([array, swap(array, axis, size, bit)], axis=0)
    return array


def reduce_chunks(array, axis, size):
    for bit in bits_of(size):
        half = array.shape[0] // 2
        array = array[:half] + swap(array[half:], axis, size, bit)
    return array


def routes(size):
    rest = bits_of(size)[1:]
    turn = len(rest) // 2
    return rest, rest[turn:] + rest[:turn]


def spread(apart, route):
    place = jnp.zeros_like(apart)
    for s, bit in enumerate(reversed(route)):
        place = place | jnp.where((apart & bit) != 0, 1 << s, 0)
    return place


def owner_of(ids, share):
    owner = ((ids.astype(f32) + 0.5) * (1.0 / share)).astype(jnp.int32)
    return owner, ids - owner * share


def right_places(ids, me, size, share):
    owner, within = owner_of(ids, share)
    return spread(owner ^ me, bits_of(size)) * share + within


def left_places(ids, me, size, share):
    owner, within = owner_of(ids, share)
    apart = owner ^ me
    half = share // 2
    quarter = size // 2 * half
    first, second = (spread(apart, route) * half for route in routes(size))
    return (apart & 1) * (2 * quarter) + jnp.where(within < half, first + within, second + within + (quarter - half))


def prep_kernel(n_row, n_col, left_share, rows, where_ref, left_ref, rel_ref, right_ref, neg_ref, ids_ref, mult_ref, bound_ref, raw_ref):
    groups, _, edges = raw_ref.shape
    n_right = mult_ref.shape[2]
    n_left = left_share * n_col
    count, me_col, me_row = where_ref[0], where_ref[1], where_ref[2]
    raw_ref[...] = jnp.zeros_like(raw_ref)
    for g in range(groups):
        for k, ref in enumerate((left_ref, rel_ref, right_ref)):
            raw_ref[g, k : k + 1, :CH] = ref[0:1, g * CH : (g + 1) * CH]
        raw_ref[g, 3:4, :CH] = neg_ref[g : g + 1, :]

    def group_step(g, carry):
        raw = raw_ref[g]
        slot = lax.broadcasted_iota(jnp.int32, (1, edges), 1)
        real = slot < CH
        valid = real & (slot + g * CH < count)
        left = jnp.where(valid, left_places(raw[0:1], me_col, n_col, left_share), n_left)
        right = right_places(raw[2:3], me_row, n_row, n_right // n_row)
        neg = jnp.where(real, right_places(raw[3:4], me_row, n_row, n_right // n_row), -1)
        key = left * edges + slot
        rows_in = [key, neg, left >> 6, left & 63, raw[1:2], right >> 6, right & 63, valid.astype(jnp.int32)]
        cols = jnp.concatenate(rows_in, axis=0).T
        payload = cols.astype(f32).astype(bf16)
        rank = jnp.zeros((8, edges), jnp.int32)
        mult = jnp.zeros((8, n_right), f32)
        bound = jnp.zeros((8, LANES), jnp.int32)
        lane_start = lax.broadcasted_iota(jnp.int32, (LANES, LANES), 1) * rows
        lane_right = lax.broadcasted_iota(jnp.int32, (LANES, n_right), 1)
        for k in range(edges // LANES):
            part = cols[k * LANES : (k + 1) * LANES]
            less = jnp.where(part[:, 0:1] < key, 1, 0)
            rank = rank + jnp.sum(less.reshape(LANES // 8, 8, edges), axis=0)
            same = jnp.where(part[:, 1:2] == lane_right, 1.0, 0.0)
            mult = mult + jnp.sum(same.reshape(LANES // 8, 8, n_right), axis=0)
            below = jnp.where(part[:, 2:3] * 64 + part[:, 3:4] < lane_start, 1, 0)
            bound = bound + jnp.sum(below.reshape(LANES // 8, 8, LANES), axis=0)
        rank = jnp.sum(rank, axis=0, keepdims=True)
        mult_ref[g] = jnp.sum(mult, axis=0, keepdims=True)
        bound_ref[g] = jnp.sum(bound, axis=0, keepdims=True)
        moved = []
        for k in range(edges // LANES):
            place = lax.broadcasted_iota(jnp.int32, (LANES, edges), 0) + k * LANES
            moved.append(dot(jnp.where(place == rank, 1.0, 0.0).astype(bf16), payload))
        moved = jnp.concatenate(moved, axis=0).T.astype(jnp.int32)
        out = [moved[2:3] * 64 + moved[3:4], moved[4:5], moved[5:6] * 64 + moved[6:7], moved[7:8]]
        ids_ref[g] = jnp.concatenate(out + out, axis=0)
        return carry

    lax.fori_loop(0, groups, group_step, 0)


def split_two(value):
    high = value.astype(bf16)
    return high, (value - high.astype(f32)).astype(bf16)


def packed_rows(rows):
    return 3 * rows + 8


def pack(value, tail):
    rows = value.shape[0]
    lane = lax.broadcasted_iota(jnp.int32, (rows, LANES), 1)
    first, second, third, fourth = (value[:, k * LANES : (k + 1) * LANES] for k in range(4))
    mixed = jnp.where(lane < tail, second, pltpu.roll(fourth, tail, 1))
    spill = 2 * tail - LANES
    last = jnp.zeros((8, LANES), f32)
    for k in range(rows // 8):
        moved = pltpu.roll(fourth[8 * k : 8 * k + 8], (spill * k + tail) % LANES, 1)
        place = lane[:8] - spill * k
        last = jnp.where((place >= 0) & (place < spill), moved, last)
    return jnp.concatenate([first, third, mixed, last], axis=0)


def unpack(value, rows, tail):
    lane = lax.broadcasted_iota(jnp.int32, (rows, LANES), 1)
    first, third, mixed = (value[k * rows : (k + 1) * rows] for k in range(3))
    last = value[3 * rows :]
    spill = 2 * tail - LANES
    turned = pltpu.roll(third, tail, 1)
    fourth = [pltpu.roll(last, (LANES - spill * k) % LANES, 1) for k in range(rows // 8)]
    fourth = jnp.where(lane < spill, jnp.concatenate(fourth, axis=0), 0.0)
    return first, jnp.where(lane < tail, mixed, turned), jnp.where(lane < tail, turned, mixed), fourth


def finish_kernel(parts, size, chunk, tail, flip, turned, where_ref, *refs):
    n_grads = sum(len(p) for p in parts)
    grads, (emb_ref, state_ref, new_ref, new_state_ref) = refs[:n_grads], refs[n_grads:]
    width = emb_ref.shape[0 if turned else 1]
    totals = [sum(grads[k][:size] for k in part) for part in parts]
    if flip:
        odd = lax.rem(where_ref[1], 2) == 1
        totals = [jnp.where(odd, totals[1], totals[0]), jnp.where(odd, totals[0], totals[1])]
    means, tiles_of = [], []
    for total in totals:
        for k in range(size // packed_rows(chunk)):
            tiles = unpack(total[k * packed_rows(chunk) : (k + 1) * packed_rows(chunk)], chunk, tail)
            squares = sum(t * t for t in tiles)
            means.append(jnp.sum(squares, axis=1, keepdims=True) / width)
            tiles_of.append(tiles)
    rows = chunk * len(means)
    mean = jnp.broadcast_to(jnp.concatenate(means, axis=0), (rows, LANES))
    state = jnp.broadcast_to(state_ref[...], (LANES, rows)).T
    accum = state + mean
    new_state_ref[...] = accum.T[0:1, :]
    rate = learn_rate / (jnp.sqrt(accum) + epsilon)
    if turned:
        tiles_of = [[jnp.concatenate(tiles, axis=0) for tiles in zip(*tiles_of)]]
        chunk = rows
    for k, tiles in enumerate(tiles_of):
        here = slice(k * chunk, (k + 1) * chunk)
        for j, tile in enumerate(tiles):
            low, high = j * LANES, min((j + 1) * LANES, width)
            if turned:
                new_ref[low:high, :] = emb_ref[low:high, :] - (rate * tile).T[: high - low]
            else:
                new_ref[here, low:high] = emb_ref[here, low:high] - (rate[here] * tile)[:, : high - low]


def finish(parts, size, chunk, tail, where, grads, embedding, state, name, flip=False, turned=False):
    vmem = pl.BlockSpec(memory_space=pltpu.VMEM)
    return pl.pallas_call(
        functools.partial(finish_kernel, parts, size, chunk, tail, flip, turned),
        in_specs=[pl.BlockSpec(memory_space=pltpu.SMEM)] + [vmem] * (len(grads) + 2),
        out_specs=[vmem, vmem],
        out_shape=[jax.ShapeDtypeStruct(embedding.shape, f32), jax.ShapeDtypeStruct((1, state.size), f32)],
        name=name,
    )(where, *grads, embedding, state.reshape(1, -1))


def dot(a, b):
    return jnp.dot(a, b, preferred_element_type=f32)


def edge_kernel(
    rows, chunk, tail, where_ref, bound_ref, ids_ref, mult_ref, own_ref, other_ref, right_ref, rel_ref,
    query_ref, c_hi_ref, c_lo_ref, near_ref, far_ref,
    rel_parts, right_t, d_hi_ref, d_lo_ref, grad_rel_ref, piece_ref,
):
    step = pl.program_id(0)
    tile = query_ref.shape[0]
    groups, _, edges = ids_ref.shape
    tiles_in_group = pl.num_programs(0) // mult_ref.shape[0]
    n_rel, wide = rel_ref.shape
    half = wide // 2
    n_own, n_right = own_ref.shape[0], right_ref.shape[0]
    n_left = 2 * n_own
    rel_rows = rel_parts.shape[0]

    @pl.when(step == 0)
    def _():
        grad_rel_ref[...] = jnp.zeros_like(grad_rel_ref)
        rel_parts[...] = jnp.zeros_like(rel_parts)
        rest = rel_ref[...]
        for part in range(3):
            piece = rest.astype(bf16)
            rel_parts[part * n_rel : (part + 1) * n_rel, :] = piece
            rest = rest - piece.astype(f32)
        right_t[...] = right_ref[...].T

    group = step // tiles_in_group
    start = group * CH + (step - group * tiles_in_group) * tile

    @pl.when(start >= where_ref[0])
    def _():
        for ref in (query_ref, c_hi_ref, c_lo_ref):
            ref[...] = jnp.zeros_like(ref)
        here = pl.ds(pl.multiple_of(step * tile, tile), tile)
        d_hi_ref[here, :] = jnp.zeros((tile, wide), bf16)
        d_lo_ref[here, :] = jnp.zeros((tile, wide), bf16)

    @pl.when(start < where_ref[0])
    def _():
        place = pl.multiple_of((step - group * tiles_in_group) * tile, tile)
        ids = ids_ref[group, :, pl.ds(place, tile)]
        all_cols = ids.T
        mult = mult_ref[group]
        absent = jnp.where(mult > 0.0, 0.0, -jnp.inf)

        def fetch(sub):
            cols = all_cols[sub * SUB : (sub + 1) * SUB]
            left_col, rel_col = cols[:, 0:1], cols[:, 1:2]
            rel_iota = lax.broadcasted_iota(jnp.int32, (SUB, rel_rows), 1) % n_rel
            rel_hot = jnp.where(rel_iota == rel_col, 1.0, 0.0).astype(bf16)
            rel_vec = dot(rel_hot, rel_parts[...])
            left_iota = lax.broadcasted_iota(jnp.int32, (SUB, n_left), 1)
            left_hot = jnp.where(left_iota == left_col, 1.0, 0.0).astype(bf16)
            left_vec = dot(left_hot[:, :n_own], own_ref[...]) + dot(left_hot[:, n_own:], other_ref[...])
            a_re, a_im = left_vec[:, :half], left_vec[:, half:]
            b_re, b_im = rel_vec[:, :half], rel_vec[:, half:]
            query = jnp.concatenate([a_re * b_re - a_im * b_im, a_re * b_im + a_im * b_re], axis=1).astype(bf16)
            query_ref[sub * SUB : (sub + 1) * SUB, :] = query
            return (a_re, a_im, b_re, b_im), dot(query, right_t[...])

        def weigh(sub, scores):
            cols = all_cols[sub * SUB : (sub + 1) * SUB]
            right_col, valid = cols[:, 2:3], cols[:, 3:4].astype(f32)
            right_iota = lax.broadcasted_iota(jnp.int32, (SUB, n_right), 1)
            is_target = right_iota == right_col
            positive = jnp.sum(jnp.where(is_target, scores, 0.0), axis=1, keepdims=True)
            masked = scores + absent
            highest = jnp.maximum(jnp.max(masked, axis=1, keepdims=True), positive)
            expo = jnp.exp(masked - highest)
            expo_pos = jnp.exp(positive - highest)
            totals = expo_pos + jnp.sum(expo * mult, axis=1, keepdims=True)
            probability = (expo * (valid / totals)).astype(bf16)
            pos_coeff = (expo_pos / totals - 1.0) * valid
            coeff = mult * probability.astype(f32) + jnp.where(is_target, pos_coeff, 0.0)
            c_hi, c_lo = split_two(coeff)
            c_hi_ref[sub * SUB : (sub + 1) * SUB, :] = c_hi
            c_lo_ref[sub * SUB : (sub + 1) * SUB, :] = c_lo
            return c_hi, c_lo

        def back(sub, parts, coeffs):
            a_re, a_im, b_re, b_im = parts
            d_query = dot(coeffs[0], right_ref[...]) + dot(coeffs[1], right_ref[...])
            g_re, g_im = d_query[:, :half], d_query[:, half:]
            d_left = jnp.concatenate([g_re * b_re + g_im * b_im, g_im * b_re - g_re * b_im], axis=1)
            d_hi, d_lo = split_two(d_left)
            here = pl.ds(pl.multiple_of(step * tile + sub * SUB, SUB), SUB)
            d_hi_ref[here, :] = d_hi
            d_lo_ref[here, :] = d_lo
            d_rel = jnp.concatenate([g_re * a_re + g_im * a_im, g_im * a_re - g_re * a_im], axis=1)
            r_hi, r_lo = split_two(d_rel)
            row_iota = lax.broadcasted_iota(jnp.int32, (n_rel, SUB), 0)
            rel_hot_t = jnp.where(row_iota == ids[1:2, sub * SUB : (sub + 1) * SUB], 1.0, 0.0).astype(bf16)
            return dot(rel_hot_t, r_hi) + dot(rel_hot_t, r_lo)

        subs = tile // SUB
        fetched, weighed, rel_total = {}, {}, 0.0
        for turn in range(subs + 2):
            if turn < subs:
                fetched[turn] = fetch(turn)
            if 0 <= turn - 1 < subs:
                weighed[turn - 1] = weigh(turn - 1, fetched[turn - 1][1])
            if 0 <= turn - 2 < subs:
                rel_total += back(turn - 2, fetched[turn - 2][0], weighed[turn - 2])
        grad_rel_ref[...] += rel_total

    @pl.when(step == pl.num_programs(0) - 1)
    def _():
        n_pieces = n_left // rows

        def hot_rows(g, base, at, size):
            row_iota = lax.broadcasted_iota(jnp.int32, (rows, size), 0) + base
            return jnp.where(row_iota == ids_ref[g, 0:1, pl.ds(at, size)], 1.0, 0.0).astype(bf16)

        def span(g, piece):
            return jnp.minimum(bound_ref[g, piece] // WINDOW * WINDOW, edges - SPAN)

        few = n_rel // 2
        odd = lax.rem(where_ref[1], 2)
        rel_size = packed_rows(few)
        near_ref[-rel_size:, :] = pack(grad_rel_ref[pl.ds(pl.multiple_of(odd * few, few), few), :], tail)
        far_ref[-rel_size:, :] = pack(grad_rel_ref[pl.ds(pl.multiple_of((1 - odd) * few, few), few), :], tail)

        def piece_step(piece, out_ref, shift):
            base = pl.multiple_of(piece * rows, rows)
            total = jnp.zeros((rows, wide), f32)
            for g in range(groups):
                at = pl.multiple_of(span(g, piece), WINDOW)
                hot = hot_rows(g, base, at, SPAN)
                here = pl.ds(pl.multiple_of(g * edges + at, WINDOW), SPAN)
                total = total + dot(hot, d_hi_ref[here, :]) + dot(hot, d_lo_ref[here, :])
            piece_ref[...] = total

            def rest_step(g, carry):
                def window_step(w, inner):
                    at = pl.multiple_of(w * WINDOW, WINDOW)
                    hot = hot_rows(g, base, at, WINDOW)
                    here = pl.ds(pl.multiple_of(g * edges + at, WINDOW), WINDOW)
                    piece_ref[...] += dot(hot, d_hi_ref[here, :]) + dot(hot, d_lo_ref[here, :])
                    return inner

                first = (span(g, piece) + SPAN) // WINDOW
                return lax.fori_loop(first, (bound_ref[g, piece + 1] + WINDOW - 1) // WINDOW, window_step, carry)

            lax.fori_loop(0, groups, rest_step, 0)
            size = packed_rows(chunk)
            for k in range(rows // chunk):
                there = pl.ds(pl.multiple_of((piece - shift) * (rows // chunk) * size + k * size, 8), size)
                out_ref[there, :] = pack(piece_ref[k * chunk : (k + 1) * chunk, :], tail)

        for shift, out_ref in ((0, near_ref), (n_pieces // 2, far_ref)):

            def each(k, carry, shift=shift, out_ref=out_ref):
                piece_step(k + shift, out_ref, shift)
                return carry

            lax.fori_loop(0, n_pieces // 2, each, 0)


def right_kernel(tail, query_ref, c_hi_ref, c_lo_ref, out_ref, total):
    step = pl.program_id(0)

    @pl.when(step == 0)
    def _():
        total[...] = jnp.zeros_like(total)

    dims = (((0,), (0,)), ((), ()))
    query = query_ref[...]
    total[...] += lax.dot_general(query, c_hi_ref[...], dims, preferred_element_type=f32) + lax.dot_general(
        query, c_lo_ref[...], dims, preferred_element_type=f32
    )

    @pl.when(step == pl.num_programs(0) - 1)
    def _():
        size = packed_rows(RIGHT_CHUNK)
        whole_sum = total[...].T
        for k in range(total.shape[1] // RIGHT_CHUNK):
            out_ref[k * size : (k + 1) * size, :] = pack(whole_sum[k * RIGHT_CHUNK : (k + 1) * RIGHT_CHUNK], tail)


def whole(shape):
    return pl.BlockSpec(shape, lambda *_: (0,) * len(shape))


def body(n_row, n_col, left_emb, left_state, right_emb, right_state, relation, rel_state, left_ids, rel_ids, right_ids, neg_ids, counts):
    width = relation.shape[1]
    half_pad = round_up(width // 2, LANES)
    wide = 2 * half_pad
    left_share, right_share = left_emb.shape[1], right_emb.shape[1]
    n_left, n_right, n_rel = left_share * n_col, right_share * n_row, relation.shape[0]
    groups = neg_ids.shape[2]
    edges = round_up(CH, TILE)
    slots = groups * edges
    tile = TILE if n_right <= SUB else SUB
    tiles = edges // tile

    smem = pl.BlockSpec(memory_space=pltpu.SMEM)
    rows = left_share * 4
    where = jnp.stack([counts[0, 0], lax.axis_index("col"), lax.axis_index("row")])

    def prepare(where, left_ids, rel_ids, right_ids, neg_ids):
        return pl.pallas_call(
            functools.partial(prep_kernel, n_row, n_col, left_share, rows),
            in_specs=[smem] + [whole((1, groups * CH))] * 3 + [whole((groups, CH))],
            out_specs=[whole((groups, 8, edges)), whole((groups, 1, n_right)), whole((groups, 1, LANES))],
            out_shape=[
                jax.ShapeDtypeStruct((groups, 8, edges), jnp.int32),
                jax.ShapeDtypeStruct((groups, 1, n_right), f32),
                jax.ShapeDtypeStruct((groups, 1, LANES), jnp.int32),
            ],
            scratch_shapes=[pltpu.VMEM((groups, 8, edges), jnp.int32)],
            cost_estimate=pl.CostEstimate(flops=16 * slots * edges, bytes_accessed=32 * slots, transcendentals=0),
            compiler_params=pltpu.CompilerParams(vmem_limit_bytes=32 << 20),
            name="prep",
        )(where, left_ids[0], rel_ids[0], right_ids[0], neg_ids[0, 0])

    rel_wide = to_halves(relation, half_pad)
    right_mine = to_halves(right_emb[0].astype(bf16), half_pad)
    mine = to_halves(left_emb[0].astype(bf16), half_pad)
    part_a, part_b = mine[: left_share // 2], mine[left_share // 2 :]
    route_a, route_b = routes(n_col)
    right_part = gather_chunks(right_mine, "row", n_row)
    for step, (bit_a, bit_b) in enumerate(zip(reversed(route_a), reversed(route_b))):
        part_a, part_b = tie(part_a, part_b)
        more_a, more_b = swap(part_a, "col", n_col, bit_a), swap(part_b, "col", n_col, bit_b)
        if step == 1:
            ids, mult, bound = prepare(*raw)
            more_a, more_b, ids, mult, bound = tie(more_a, more_b, ids, mult, bound)
        else:
            more_a, more_b = tie(more_a, more_b)
        part_a = jnp.concatenate([part_a, more_a], axis=0)
        part_b = jnp.concatenate([part_b, more_b], axis=0)
        if step == 0:
            part_a, part_b, *raw = tie(part_a, part_b, where, left_ids, rel_ids, right_ids, neg_ids)
    own = jnp.concatenate([part_a, part_b], axis=0)
    bound = bound.reshape(groups, LANES)
    own, ids, mult, bound, right_part, rel_wide = tie(own, ids, mult, bound, right_part, rel_wide)
    other = swap(own, "col", n_col, 1)

    tile_block = lambda lanes: pl.BlockSpec((tile, lanes), lambda i: (i, 0))
    chunk, tail = left_share // 2, width // 2 - LANES
    packed_half = n_left // 2 // chunk * packed_rows(chunk)
    packed_rel = packed_rows(n_rel // 2)
    query, c_hi, c_lo, near, far = pl.pallas_call(
        functools.partial(edge_kernel, rows, chunk, tail),
        grid=(groups * tiles,),
        in_specs=[
            smem,
            smem,
            whole((groups, 8, edges)),
            whole((groups, 1, n_right)),
            whole((n_left // 2, wide)),
            whole((n_left // 2, wide)),
            whole((n_right, wide)),
            whole((n_rel, wide)),
        ],
        out_specs=[
            tile_block(wide),
            tile_block(n_right),
            tile_block(n_right),
            whole((packed_half + packed_rel, LANES)),
            whole((packed_half + packed_rel, LANES)),
        ],
        out_shape=[
            jax.ShapeDtypeStruct((slots, wide), bf16),
            jax.ShapeDtypeStruct((slots, n_right), bf16),
            jax.ShapeDtypeStruct((slots, n_right), bf16),
            jax.ShapeDtypeStruct((packed_half + packed_rel, LANES), f32),
            jax.ShapeDtypeStruct((packed_half + packed_rel, LANES), f32),
        ],
        scratch_shapes=[
            pltpu.VMEM((round_up(3 * n_rel, LANES), wide), bf16),
            pltpu.VMEM((wide, n_right), bf16),
            pltpu.VMEM((slots, wide), bf16),
            pltpu.VMEM((slots, wide), bf16),
            pltpu.VMEM((n_rel, wide), f32),
            pltpu.VMEM((rows, wide), f32),
        ],
        compiler_params=pltpu.CompilerParams(vmem_limit_bytes=56 << 20),
        name="edges",
    )(where, bound, ids, mult, own, other, right_part, rel_wide)

    packed_right = n_right // RIGHT_CHUNK * packed_rows(RIGHT_CHUNK)

    def right_sum(query, c_hi, c_lo):
        group_block = lambda lanes: pl.BlockSpec((edges, lanes), lambda i: (i, 0))
        return pl.pallas_call(
            functools.partial(right_kernel, tail),
            grid=(groups,),
            in_specs=[group_block(wide), group_block(n_right), group_block(n_right)],
            out_specs=whole((packed_right, LANES)),
            out_shape=jax.ShapeDtypeStruct((packed_right, LANES), f32),
            scratch_shapes=[pltpu.VMEM((wide, n_right), f32)],
            compiler_params=pltpu.CompilerParams(vmem_limit_bytes=48 << 20),
            cost_estimate=pl.CostEstimate(flops=4 * slots * wide * n_right, bytes_accessed=6 * slots * wide, transcendentals=0),
            name="right_sum",
        )(query, c_hi, c_lo)

    come = swap(far, "col", n_col, 1)
    half = packed_half // 2
    sum_a, sum_b = near[:half] + come[:half], near[half : 2 * half] + come[half : 2 * half]
    grad_rel = near[2 * half :] + come[2 * half :]
    sum_a, sum_b, grad_rel, query, c_hi, c_lo = tie(sum_a, sum_b, grad_rel, query, c_hi, c_lo)
    stages = len(route_a)
    carried = [route_a[k] if k % 2 else route_b[k] for k in range(1, stages)]
    alone = [("col", n_col, bit) for bit in route_a if bit not in carried]
    half = half // 2
    more_a, more_b = swap(sum_a[half:], "col", n_col, route_a[0]), swap(sum_b[half:], "col", n_col, route_b[0])
    for step in [("row", n_row, bit) for bit in bits_of(n_row)] + alone[:-1]:
        grad_rel = grad_rel + swap(grad_rel, *step)
    grad_rel, query, c_hi, c_lo = tie(grad_rel, query, c_hi, c_lo)
    more_rel = swap(grad_rel, *alone[-1])
    more_a, more_b, more_rel, grad_right = tie(more_a, more_b, more_rel, right_sum(query, c_hi, c_lo))
    sum_a, sum_b, grad_rel, grad_right = tie(sum_a[:half] + more_a, sum_b[:half] + more_b, grad_rel + more_rel, grad_right)
    for stage in range(1, stages):
        half = sum_b.shape[0] // 2
        far_a, far_b = sum_a[half:], sum_b[half:]
        if stage % 2:
            far_a = jnp.concatenate([far_a, grad_rel], axis=0)
        else:
            far_b = jnp.concatenate([far_b, grad_rel], axis=0)
        more_a, more_b = swap(far_a, "col", n_col, route_a[stage]), swap(far_b, "col", n_col, route_b[stage])
        if stage == 1:
            more_a, more_b, grad_right = tie(more_a, more_b, reduce_chunks(grad_right, "row", n_row))
        elif stage == 2:
            new_right, new_right_state = finish(
                ((0,),), packed_right // n_row, RIGHT_CHUNK, tail, where, (grad_right,), right_emb[0].T, right_state, "new_right", turned=True
            )
            more_a, more_b, new_right, new_right_state = tie(more_a, more_b, new_right, new_right_state)
        grad_rel = grad_rel + (more_a if stage % 2 else more_b)[half:]
        if stage < stages - 1:
            sum_a, sum_b, grad_rel = tie(sum_a[:half] + more_a[:half], sum_b[:half] + more_b[:half], grad_rel)
    other_rel = swap(grad_rel, "col", n_col, 1)
    new_left, new_left_state = finish(
        ((0, 1), (2, 3)), half, chunk, tail, where, (sum_a, more_a, sum_b, more_b), left_emb[0], left_state, "new_left"
    )
    new_rel, new_rel_state = finish(
        ((0,), (1,)), packed_rel, n_rel // 2, tail, where, (grad_rel, other_rel), relation, rel_state, "new_rel", flip=True
    )
    return new_left[None], new_left_state, new_right.T[None], new_right_state, new_rel, new_rel_state[0]


def solution(mesh):
    entities = (P("row", "col", None), P("row", "col"), P("col", "row", None), P("col", "row"), P(), P())
    return jax.shard_map(
        functools.partial(body, mesh.shape["row"], mesh.shape["col"]),
        mesh=mesh,
        in_specs=entities + (P("row", "col", None),) * 3 + (P("row", "col", None, None), P("row", "col")),
        out_specs=entities,
        check_vma=False,
    )
```

```python
import functools

import jax
import jax.numpy as jnp
from jax import lax
from jax.experimental import pallas as pl
from jax.experimental.pallas import tpu as pltpu
from jax.sharding import PartitionSpec as P

CH = 1000
LANES = 128
TILE = 1024
SUB = 512
WINDOW = 128
SPAN = 512
RIGHT_CHUNK = 64
THIRDS = 64

learn_rate = 0.1
epsilon = 1e-10
bf16 = jnp.bfloat16
f32 = jnp.float32


def round_up(value, step):
    return (value + step - 1) // step * step


def to_halves(array, half_pad):
    half = array.shape[-1] // 2
    pad = [(0, 0)] * (array.ndim - 1) + [(0, half_pad - half)]
    return jnp.concatenate([jnp.pad(array[..., :half], pad), jnp.pad(array[..., half:], pad)], axis=-1)


def from_halves(array, width):
    half_pad = array.shape[-1] // 2
    return jnp.concatenate([array[..., : width // 2], array[..., half_pad : half_pad + width // 2]], axis=-1)


def bits_of(size):
    return [1 << b for b in range(size.bit_length() - 1)]


def swap(array, axis, size, bit):
    return lax.ppermute(array, axis, [(i, i ^ bit) for i in range(size)])


def tie(*arrays):
    return lax.optimization_barrier(arrays)


def gather_chunks(array, axis, size):
    for bit in reversed(bits_of(size)):
        array = jnp.concatenate([array, swap(array, axis, size, bit)], axis=0)
    return array


def reduce_chunks(array, axis, size, skip=0):
    for bit in bits_of(size)[skip:]:
        half = array.shape[0] // 2
        array = array[:half] + swap(array[half:], axis, size, bit)
    return array


def routes(size):
    rest = bits_of(size)[1:]
    turn = len(rest) // 2
    return rest, rest[turn:] + rest[:turn]


def spread(apart, route):
    place = jnp.zeros_like(apart)
    for s, bit in enumerate(reversed(route)):
        place = place | jnp.where((apart & bit) != 0, 1 << s, 0)
    return place


def owner_of(ids, share):
    owner = ((ids.astype(f32) + 0.5) * (1.0 / share)).astype(jnp.int32)
    return owner, ids - owner * share


def right_places(ids, me, size, share):
    owner, within = owner_of(ids, share)
    return spread(owner ^ me, bits_of(size)) * share + within


def left_places(ids, me, size, share):
    owner, within = owner_of(ids, share)
    apart = owner ^ me
    half = share // 2
    quarter = size // 2 * half
    first, second = (spread(apart, route) * half for route in routes(size))
    return (apart & 1) * (2 * quarter) + jnp.where(within < half, first + within, second + within + (quarter - half))


def prep_kernel(n_row, n_col, left_share, rows, where_ref, left_ref, rel_ref, right_ref, neg_ref, ids_ref, mult_ref, bound_ref, raw_ref):
    groups, _, edges = raw_ref.shape
    n_right = mult_ref.shape[2]
    n_left = left_share * n_col
    count, me_col, me_row = where_ref[0], where_ref[1], where_ref[2]
    raw_ref[...] = jnp.zeros_like(raw_ref)
    for g in range(groups):
        for k, ref in enumerate((left_ref, rel_ref, right_ref)):
            raw_ref[g, k : k + 1, :CH] = ref[0:1, g * CH : (g + 1) * CH]
        raw_ref[g, 3:4, :CH] = neg_ref[g : g + 1, :]

    def group_step(g, carry):
        raw = raw_ref[g]
        slot = lax.broadcasted_iota(jnp.int32, (1, edges), 1)
        real = slot < CH
        valid = real & (slot + g * CH < count)
        left = jnp.where(valid, left_places(raw[0:1], me_col, n_col, left_share), n_left)
        right = right_places(raw[2:3], me_row, n_row, n_right // n_row)
        neg = jnp.where(real, right_places(raw[3:4], me_row, n_row, n_right // n_row), -1)
        key = left * edges + slot
        rows_in = [key, neg, left >> 6, left & 63, raw[1:2], right >> 6, right & 63, valid.astype(jnp.int32)]
        cols = jnp.concatenate(rows_in, axis=0).T
        payload = cols.astype(f32).astype(bf16)
        rank = jnp.zeros((8, edges), jnp.int32)
        mult = jnp.zeros((8, n_right), f32)
        bound = jnp.zeros((8, LANES), jnp.int32)
        lane = lax.broadcasted_iota(jnp.int32, (LANES, LANES), 1)
        lane_start = jnp.where(lane < THIRDS, lane * rows, (lane - THIRDS) * (n_left // 3))
        lane_right = lax.broadcasted_iota(jnp.int32, (LANES, n_right), 1)
        for k in range(edges // LANES):
            part = cols[k * LANES : (k + 1) * LANES]
            less = jnp.where(part[:, 0:1] < key, 1, 0)
            rank = rank + jnp.sum(less.reshape(LANES // 8, 8, edges), axis=0)
            same = jnp.where(part[:, 1:2] == lane_right, 1.0, 0.0)
            mult = mult + jnp.sum(same.reshape(LANES // 8, 8, n_right), axis=0)
            below = jnp.where(part[:, 2:3] * 64 + part[:, 3:4] < lane_start, 1, 0)
            bound = bound + jnp.sum(below.reshape(LANES // 8, 8, LANES), axis=0)
        rank = jnp.sum(rank, axis=0, keepdims=True)
        mult_ref[g] = jnp.sum(mult, axis=0, keepdims=True)
        bound_ref[g] = jnp.sum(bound, axis=0, keepdims=True)
        moved = []
        for k in range(edges // LANES):
            place = lax.broadcasted_iota(jnp.int32, (LANES, edges), 0) + k * LANES
            moved.append(dot(jnp.where(place == rank, 1.0, 0.0).astype(bf16), payload))
        moved = jnp.concatenate(moved, axis=0).T.astype(jnp.int32)
        out = [moved[2:3] * 64 + moved[3:4], moved[4:5], moved[5:6] * 64 + moved[6:7], moved[7:8]]
        ids_ref[g] = jnp.concatenate(out + out, axis=0)
        return carry

    lax.fori_loop(0, groups, group_step, 0)


def split_two(value):
    high = value.astype(bf16)
    return high, (value - high.astype(f32)).astype(bf16)


def packed_rows(rows):
    return 3 * rows + 8


def pack(value, tail):
    rows = value.shape[0]
    lane = lax.broadcasted_iota(jnp.int32, (rows, LANES), 1)
    first, second, third, fourth = (value[:, k * LANES : (k + 1) * LANES] for k in range(4))
    mixed = jnp.where(lane < tail, second, pltpu.roll(fourth, tail, 1))
    spill = 2 * tail - LANES
    last = jnp.zeros((8, LANES), f32)
    for k in range(rows // 8):
        moved = pltpu.roll(fourth[8 * k : 8 * k + 8], (spill * k + tail) % LANES, 1)
        place = lane[:8] - spill * k
        last = jnp.where((place >= 0) & (place < spill), moved, last)
    return jnp.concatenate([first, third, mixed, last], axis=0)


def unpack(value, rows, tail):
    lane = lax.broadcasted_iota(jnp.int32, (rows, LANES), 1)
    first, third, mixed = (value[k * rows : (k + 1) * rows] for k in range(3))
    last = value[3 * rows :]
    spill = 2 * tail - LANES
    turned = pltpu.roll(third, tail, 1)
    fourth = [pltpu.roll(last, (LANES - spill * k) % LANES, 1) for k in range(rows // 8)]
    fourth = jnp.where(lane < spill, jnp.concatenate(fourth, axis=0), 0.0)
    return first, jnp.where(lane < tail, mixed, turned), jnp.where(lane < tail, turned, mixed), fourth


def finish_rows(job, tail, where_ref, grads, emb_ref, state_ref, new_ref, new_state_ref):
    parts, size, chunk, flip, turned = job
    width = emb_ref.shape[0 if turned else 1]
    totals = [sum(grads[k][start : start + size] for k, start in part) for part in parts]
    if flip:
        odd = lax.rem(where_ref[1], 2) == 1
        totals = [jnp.where(odd, totals[1], totals[0]), jnp.where(odd, totals[0], totals[1])]
    means, tiles_of = [], []
    for total in totals:
        for k in range(size // packed_rows(chunk)):
            tiles = unpack(total[k * packed_rows(chunk) : (k + 1) * packed_rows(chunk)], chunk, tail)
            squares = sum(t * t for t in tiles)
            means.append(jnp.sum(squares, axis=1, keepdims=True) / width)
            tiles_of.append(tiles)
    rows = chunk * len(means)
    mean = jnp.broadcast_to(jnp.concatenate(means, axis=0), (rows, LANES))
    state = jnp.broadcast_to(state_ref[...], (LANES, rows)).T
    accum = state + mean
    new_state_ref[...] = accum.T[0:1, :]
    rate = learn_rate / (jnp.sqrt(accum) + epsilon)
    if turned:
        tiles_of = [[jnp.concatenate(tiles, axis=0) for tiles in zip(*tiles_of)]]
        chunk = rows
    for k, tiles in enumerate(tiles_of):
        here = slice(k * chunk, (k + 1) * chunk)
        for j, tile in enumerate(tiles):
            low, high = j * LANES, min((j + 1) * LANES, width)
            if turned:
                new_ref[low:high, :] = emb_ref[low:high, :] - (rate * tile).T[: high - low]
            else:
                new_ref[here, low:high] = emb_ref[here, low:high] - (rate[here] * tile)[:, : high - low]


def finish_kernel(jobs, tail, n_grads, where_ref, *refs):
    grads, ins, outs = refs[:n_grads], refs[n_grads : n_grads + 2 * len(jobs)], refs[n_grads + 2 * len(jobs) :]
    for k, job in enumerate(jobs):
        finish_rows(job, tail, where_ref, grads, *ins[2 * k : 2 * k + 2], *outs[2 * k : 2 * k + 2])


def finish(jobs, tail, where, grads, tables, name):
    vmem = pl.BlockSpec(memory_space=pltpu.VMEM)
    shapes, operands = [], []
    for embedding, state in tables:
        operands += [embedding, state.reshape(1, -1)]
        shapes += [jax.ShapeDtypeStruct(embedding.shape, f32), jax.ShapeDtypeStruct((1, state.size), f32)]
    return pl.pallas_call(
        functools.partial(finish_kernel, jobs, tail, len(grads)),
        in_specs=[pl.BlockSpec(memory_space=pltpu.SMEM)] + [vmem] * (len(grads) + len(operands)),
        out_specs=[vmem] * len(shapes),
        out_shape=shapes,
        name=name,
    )(where, *grads, *operands)


def dot(a, b):
    return jnp.dot(a, b, preferred_element_type=f32)


def edge_kernel(
    rows, chunk, tail, where_ref, bound_ref, ids_ref, mult_ref, own_ref, other_ref, right_ref, right_t, rel_ref,
    query_ref, c_hi_ref, c_lo_ref, near_ref, far_ref,
    rel_parts, d_hi_ref, d_lo_ref, grad_rel_ref, piece_ref,
):
    step = pl.program_id(0)
    tile = query_ref.shape[0]
    groups, _, edges = ids_ref.shape
    tiles_in_group = pl.num_programs(0) // mult_ref.shape[0]
    n_rel, wide = rel_ref.shape
    half = wide // 2
    n_own, n_right = own_ref.shape[0], right_ref.shape[0]
    n_left = 2 * n_own
    rel_rows = rel_parts.shape[0]

    @pl.when(step == 0)
    def _():
        grad_rel_ref[...] = jnp.zeros_like(grad_rel_ref)
        rel_parts[...] = jnp.zeros_like(rel_parts)
        rest = rel_ref[...]
        for part in range(3):
            piece = rest.astype(bf16)
            rel_parts[part * n_rel : (part + 1) * n_rel, :] = piece
            rest = rest - piece.astype(f32)

    group = step // tiles_in_group
    start = group * CH + (step - group * tiles_in_group) * tile

    @pl.when(start >= where_ref[0])
    def _():
        for ref in (query_ref, c_hi_ref, c_lo_ref):
            ref[...] = jnp.zeros_like(ref)
        here = pl.ds(pl.multiple_of(step * tile, tile), tile)
        d_hi_ref[here, :] = jnp.zeros((tile, wide), bf16)
        d_lo_ref[here, :] = jnp.zeros((tile, wide), bf16)

    def run(spans):
        place = pl.multiple_of((step - group * tiles_in_group) * tile, tile)
        ids = ids_ref[group, :, pl.ds(place, tile)]
        all_cols = ids.T
        mult = mult_ref[group]
        absent = jnp.where(mult > 0.0, 0.0, -jnp.inf)

        def fetch(sub):
            cols = all_cols[sub * SUB : (sub + 1) * SUB]
            left_col, rel_col = cols[:, 0:1], cols[:, 1:2]
            rel_iota = lax.broadcasted_iota(jnp.int32, (SUB, rel_rows), 1) % n_rel
            rel_hot = jnp.where(rel_iota == rel_col, 1.0, 0.0).astype(bf16)
            rel_vec = dot(rel_hot, rel_parts[...])
            low, high = spans[sub]
            left_iota = lax.broadcasted_iota(jnp.int32, (SUB, high - low), 1) + low
            left_hot = jnp.where(left_iota == left_col, 1.0, 0.0).astype(bf16)
            left_vec = dot(left_hot[:, : n_own - low], own_ref[low:, :]) + dot(left_hot[:, n_own - low :], other_ref[: high - n_own, :])
            a_re, a_im = left_vec[:, :half], left_vec[:, half:]
            b_re, b_im = rel_vec[:, :half], rel_vec[:, half:]
            query = jnp.concatenate([a_re * b_re - a_im * b_im, a_re * b_im + a_im * b_re], axis=1).astype(bf16)
            query_ref[sub * SUB : (sub + 1) * SUB, :] = query
            return (a_re, a_im, b_re, b_im), dot(query, right_t[...])

        def weigh(sub, scores):
            cols = all_cols[sub * SUB : (sub + 1) * SUB]
            right_col, valid = cols[:, 2:3], cols[:, 3:4].astype(f32)
            right_iota = lax.broadcasted_iota(jnp.int32, (SUB, n_right), 1)
            is_target = right_iota == right_col
            positive = jnp.sum(jnp.where(is_target, scores, 0.0), axis=1, keepdims=True)
            masked = scores + absent
            highest = jnp.maximum(jnp.max(masked, axis=1, keepdims=True), positive)
            expo = jnp.exp(masked - highest)
            expo_pos = jnp.exp(positive - highest)
            totals = expo_pos + jnp.sum(expo * mult, axis=1, keepdims=True)
            probability = (expo * (valid / totals)).astype(bf16)
            pos_coeff = (expo_pos / totals - 1.0) * valid
            coeff = mult * probability.astype(f32) + jnp.where(is_target, pos_coeff, 0.0)
            c_hi, c_lo = split_two(coeff)
            c_hi_ref[sub * SUB : (sub + 1) * SUB, :] = c_hi
            c_lo_ref[sub * SUB : (sub + 1) * SUB, :] = c_lo
            return c_hi, c_lo

        def back(sub, parts, coeffs):
            a_re, a_im, b_re, b_im = parts
            d_query = dot(coeffs[0], right_ref[...]) + dot(coeffs[1], right_ref[...])
            g_re, g_im = d_query[:, :half], d_query[:, half:]
            d_left = jnp.concatenate([g_re * b_re + g_im * b_im, g_im * b_re - g_re * b_im], axis=1)
            d_hi, d_lo = split_two(d_left)
            here = pl.ds(pl.multiple_of(step * tile + sub * SUB, SUB), SUB)
            d_hi_ref[here, :] = d_hi
            d_lo_ref[here, :] = d_lo
            d_rel = jnp.concatenate([g_re * a_re + g_im * a_im, g_im * a_re - g_re * a_im], axis=1)
            r_hi, r_lo = split_two(d_rel)
            row_iota = lax.broadcasted_iota(jnp.int32, (n_rel, SUB), 0)
            rel_hot_t = jnp.where(row_iota == ids[1:2, sub * SUB : (sub + 1) * SUB], 1.0, 0.0).astype(bf16)
            return dot(rel_hot_t, r_hi) + dot(rel_hot_t, r_lo)

        fetched, weighed, rel_total = {}, {}, 0.0
        for turn in range(len(spans) + 2):
            if turn < len(spans):
                fetched[turn] = fetch(turn)
            if 0 <= turn - 1 < len(spans):
                weighed[turn - 1] = weigh(turn - 1, fetched[turn - 1][1])
            if 0 <= turn - 2 < len(spans):
                rel_total += back(turn - 2, fetched[turn - 2][0], weighed[turn - 2])
        grad_rel_ref[...] += rel_total

    active = start < where_ref[0]
    subs = tile // SUB
    third = n_left // 3
    if subs == 2 and tile == edges and third % LANES == 0:
        narrow = (bound_ref[group, THIRDS + 2] >= SUB) & (bound_ref[group, THIRDS + 1] <= SUB)

        @pl.when(active & narrow)
        def _():
            run(((0, 2 * third), (third, n_left)))

        active = active & jnp.logical_not(narrow)

    @pl.when(active)
    def _():
        run(((0, n_left),) * subs)

    @pl.when(step == pl.num_programs(0) - 1)
    def _():
        n_pieces = n_left // rows

        def hot_rows(g, base, at, size):
            row_iota = lax.broadcasted_iota(jnp.int32, (rows, size), 0) + base
            return jnp.where(row_iota == ids_ref[g, 0:1, pl.ds(at, size)], 1.0, 0.0).astype(bf16)

        def span(g, piece):
            return jnp.minimum(bound_ref[g, piece] // WINDOW * WINDOW, edges - SPAN)

        few = n_rel // 2
        odd = lax.rem(where_ref[1], 2)
        rel_size = packed_rows(few)
        near_ref[-rel_size:, :] = pack(grad_rel_ref[pl.ds(pl.multiple_of(odd * few, few), few), :], tail)
        far_ref[-rel_size:, :] = pack(grad_rel_ref[pl.ds(pl.multiple_of((1 - odd) * few, few), few), :], tail)

        def piece_step(piece, out_ref, shift):
            base = pl.multiple_of(piece * rows, rows)
            total = jnp.zeros((rows, wide), f32)
            for g in range(groups):
                at = pl.multiple_of(span(g, piece), WINDOW)
                hot = hot_rows(g, base, at, SPAN)
                here = pl.ds(pl.multiple_of(g * edges + at, WINDOW), SPAN)
                total = total + dot(hot, d_hi_ref[here, :]) + dot(hot, d_lo_ref[here, :])
            piece_ref[...] = total

            def rest_step(g, carry):
                def window_step(w, inner):
                    at = pl.multiple_of(w * WINDOW, WINDOW)
                    hot = hot_rows(g, base, at, WINDOW)
                    here = pl.ds(pl.multiple_of(g * edges + at, WINDOW), WINDOW)
                    piece_ref[...] += dot(hot, d_hi_ref[here, :]) + dot(hot, d_lo_ref[here, :])
                    return inner

                first = (span(g, piece) + SPAN) // WINDOW
                return lax.fori_loop(first, (bound_ref[g, piece + 1] + WINDOW - 1) // WINDOW, window_step, carry)

            lax.fori_loop(0, groups, rest_step, 0)
            size = packed_rows(chunk)
            for k in range(rows // chunk):
                there = pl.ds(pl.multiple_of((piece - shift) * (rows // chunk) * size + k * size, 8), size)
                out_ref[there, :] = pack(piece_ref[k * chunk : (k + 1) * chunk, :], tail)

        for shift, out_ref in ((0, near_ref), (n_pieces // 2, far_ref)):

            def each(k, carry, shift=shift, out_ref=out_ref):
                piece_step(k + shift, out_ref, shift)
                return carry

            lax.fori_loop(0, n_pieces // 2, each, 0)


def right_kernel(tail, query_ref, c_hi_ref, c_lo_ref, out_ref, total):
    step = pl.program_id(0)

    @pl.when(step == 0)
    def _():
        total[...] = jnp.zeros_like(total)

    dims = (((0,), (0,)), ((), ()))
    query = query_ref[...]
    total[...] += lax.dot_general(query, c_hi_ref[...], dims, preferred_element_type=f32) + lax.dot_general(
        query, c_lo_ref[...], dims, preferred_element_type=f32
    )

    @pl.when(step == pl.num_programs(0) - 1)
    def _():
        size = packed_rows(RIGHT_CHUNK)
        whole_sum = total[...].T
        for k in range(total.shape[1] // RIGHT_CHUNK):
            out_ref[k * size : (k + 1) * size, :] = pack(whole_sum[k * RIGHT_CHUNK : (k + 1) * RIGHT_CHUNK], tail)


def whole(shape):
    return pl.BlockSpec(shape, lambda *_: (0,) * len(shape))


def body(n_row, n_col, left_emb, left_state, right_emb, right_state, relation, rel_state, left_ids, rel_ids, right_ids, neg_ids, counts):
    width = relation.shape[1]
    half_pad = round_up(width // 2, LANES)
    wide = 2 * half_pad
    left_share, right_share = left_emb.shape[1], right_emb.shape[1]
    n_left, n_right, n_rel = left_share * n_col, right_share * n_row, relation.shape[0]
    groups = neg_ids.shape[2]
    edges = round_up(CH, TILE)
    slots = groups * edges
    tile = TILE if n_right <= SUB else SUB
    tiles = edges // tile

    smem = pl.BlockSpec(memory_space=pltpu.SMEM)
    rows = left_share * 4
    where = jnp.stack([counts[0, 0], lax.axis_index("col"), lax.axis_index("row")])

    def prepare(where, left_ids, rel_ids, right_ids, neg_ids):
        return pl.pallas_call(
            functools.partial(prep_kernel, n_row, n_col, left_share, rows),
            in_specs=[smem] + [whole((1, groups * CH))] * 3 + [whole((groups, CH))],
            out_specs=[whole((groups, 8, edges)), whole((groups, 1, n_right)), whole((groups, 1, LANES))],
            out_shape=[
                jax.ShapeDtypeStruct((groups, 8, edges), jnp.int32),
                jax.ShapeDtypeStruct((groups, 1, n_right), f32),
                jax.ShapeDtypeStruct((groups, 1, LANES), jnp.int32),
            ],
            scratch_shapes=[pltpu.VMEM((groups, 8, edges), jnp.int32)],
            cost_estimate=pl.CostEstimate(flops=16 * slots * edges, bytes_accessed=32 * slots, transcendentals=0),
            compiler_params=pltpu.CompilerParams(vmem_limit_bytes=32 << 20),
            name="prep",
        )(where, left_ids[0], rel_ids[0], right_ids[0], neg_ids[0, 0])

    rel_wide = to_halves(relation, half_pad)
    right_mine = to_halves(right_emb[0].astype(bf16), half_pad)
    mine = to_halves(left_emb[0].astype(bf16), half_pad)
    part_a, part_b = mine[: left_share // 2], mine[left_share // 2 :]
    route_a, route_b = routes(n_col)
    right_part = gather_chunks(right_mine, "row", n_row)
    for step, (bit_a, bit_b) in enumerate(zip(reversed(route_a), reversed(route_b))):
        part_a, part_b = tie(part_a, part_b)
        more_a, more_b = swap(part_a, "col", n_col, bit_a), swap(part_b, "col", n_col, bit_b)
        if step == 1:
            ids, mult, bound = prepare(*raw)
            more_a, more_b, ids, mult, bound = tie(more_a, more_b, ids, mult, bound)
        else:
            more_a, more_b = tie(more_a, more_b)
        part_a = jnp.concatenate([part_a, more_a], axis=0)
        part_b = jnp.concatenate([part_b, more_b], axis=0)
        if step == 0:
            part_a, part_b, *raw = tie(part_a, part_b, where, left_ids, rel_ids, right_ids, neg_ids)
    own = jnp.concatenate([part_a, part_b], axis=0)
    bound = bound.reshape(groups, LANES)
    own, ids, mult, bound, right_part, rel_wide = tie(own, ids, mult, bound, right_part, rel_wide)
    other = swap(own, "col", n_col, 1)

    tile_block = lambda lanes: pl.BlockSpec((tile, lanes), lambda i: (i, 0))
    chunk, tail = left_share // 2, width // 2 - LANES
    packed_half = n_left // 2 // chunk * packed_rows(chunk)
    packed_rel = packed_rows(n_rel // 2)
    query, c_hi, c_lo, near, far = pl.pallas_call(
        functools.partial(edge_kernel, rows, chunk, tail),
        grid=(groups * tiles,),
        in_specs=[
            smem,
            smem,
            whole((groups, 8, edges)),
            whole((groups, 1, n_right)),
            whole((n_left // 2, wide)),
            whole((n_left // 2, wide)),
            whole((n_right, wide)),
            whole((wide, n_right)),
            whole((n_rel, wide)),
        ],
        out_specs=[
            tile_block(wide),
            tile_block(n_right),
            tile_block(n_right),
            whole((packed_half + packed_rel, LANES)),
            whole((packed_half + packed_rel, LANES)),
        ],
        out_shape=[
            jax.ShapeDtypeStruct((slots, wide), bf16),
            jax.ShapeDtypeStruct((slots, n_right), bf16),
            jax.ShapeDtypeStruct((slots, n_right), bf16),
            jax.ShapeDtypeStruct((packed_half + packed_rel, LANES), f32),
            jax.ShapeDtypeStruct((packed_half + packed_rel, LANES), f32),
        ],
        scratch_shapes=[
            pltpu.VMEM((round_up(3 * n_rel, LANES), wide), bf16),
            pltpu.VMEM((slots, wide), bf16),
            pltpu.VMEM((slots, wide), bf16),
            pltpu.VMEM((n_rel, wide), f32),
            pltpu.VMEM((rows, wide), f32),
        ],
        compiler_params=pltpu.CompilerParams(vmem_limit_bytes=56 << 20),
        name="edges",
    )(where, bound, ids, mult, own, other, right_part, right_part.T, rel_wide)

    packed_right = n_right // RIGHT_CHUNK * packed_rows(RIGHT_CHUNK)

    def right_sum(part, query, c_hi, c_lo):
        return pl.pallas_call(
            functools.partial(right_kernel, tail),
            grid=(groups,),
            in_specs=[pl.BlockSpec((edges, wide), lambda i: (i, 0))] + [pl.BlockSpec((edges, n_right // 2), lambda i: (i, part))] * 2,
            out_specs=whole((packed_right // 2, LANES)),
            out_shape=jax.ShapeDtypeStruct((packed_right // 2, LANES), f32),
            scratch_shapes=[pltpu.VMEM((wide, n_right // 2), f32)],
            compiler_params=pltpu.CompilerParams(vmem_limit_bytes=48 << 20),
            cost_estimate=pl.CostEstimate(flops=2 * slots * wide * n_right, bytes_accessed=4 * slots * wide, transcendentals=0),
            name="right_sum",
        )(query, c_hi, c_lo)

    come, near, far_right, query, c_hi, c_lo = tie(
        swap(far, "col", n_col, 1), near, right_sum(1, query, c_hi, c_lo), query, c_hi, c_lo
    )
    half = packed_half // 2
    sum_a, sum_b = near[:half] + come[:half], near[half : 2 * half] + come[half : 2 * half]
    grad_rel = near[2 * half :] + come[2 * half :]
    sum_a, sum_b, grad_rel, query, c_hi, c_lo = tie(sum_a, sum_b, grad_rel, query, c_hi, c_lo)
    stages = len(route_a)
    carried = [route_a[k] if k % 2 else route_b[k] for k in range(1, stages)]
    alone = [("col", n_col, bit) for bit in route_a if bit not in carried]
    half = half // 2
    more_a, more_b = swap(sum_a[half:], "col", n_col, route_a[0]), swap(sum_b[half:], "col", n_col, route_b[0])
    lone = [("row", n_row, bit) for bit in bits_of(n_row)] + alone[:-1]
    for step in lone[:-1]:
        grad_rel = grad_rel + swap(grad_rel, *step)
    grad_rel, query, c_hi, c_lo = tie(grad_rel + swap(grad_rel, *lone[-1]), query, c_hi, c_lo)
    more_rel = swap(grad_rel, *alone[-1])
    come_right = swap(far_right, "row", n_row, 1)
    more_a, more_b, more_rel, near_right = tie(more_a, more_b, more_rel, right_sum(0, query, c_hi, c_lo))
    sum_a, sum_b, grad_rel, near_right = tie(sum_a[:half] + more_a, sum_b[:half] + more_b, grad_rel + more_rel, near_right)
    for stage in range(1, stages):
        half = sum_b.shape[0] // 2
        far_a, far_b = sum_a[half:], sum_b[half:]
        if stage % 2:
            far_a = jnp.concatenate([far_a, grad_rel], axis=0)
        else:
            far_b = jnp.concatenate([far_b, grad_rel], axis=0)
        more_a, more_b = swap(far_a, "col", n_col, route_a[stage]), swap(far_b, "col", n_col, route_b[stage])
        if stage == stages - 1:
            other_rel = swap(grad_rel, "col", n_col, 1)
            cross_rel = swap(grad_rel, "col", n_col, carried[-1] | 1)
            more_a, more_b, other_rel, cross_rel = tie(more_a, more_b, other_rel, cross_rel)
        if stage == 1:
            more_a, more_b, grad_right = tie(
                more_a, more_b, reduce_chunks(near_right + come_right, "row", n_row, skip=1)
            )
        elif stage == 2:
            job = (((0, 0),),), packed_right // n_row, RIGHT_CHUNK, False, True
            new_right, new_right_state = finish((job,), tail, where, (grad_right,), ((right_emb[0].T, right_state),), "new_right")
            more_a, more_b, new_right, new_right_state = tie(more_a, more_b, new_right, new_right_state)
        if stage < stages - 1:
            grad_rel = grad_rel + (more_a if stage % 2 else more_b)[half:]
            sum_a, sum_b, grad_rel = tie(sum_a[:half] + more_a[:half], sum_b[:half] + more_b[:half], grad_rel)
    jobs = (
        (((0, 0), (1, 0)), ((2, 0), (3, 0))), half, chunk, False, False
    ), (
        (((4, 0), (1 if stage % 2 else 3, half)), ((5, 0), (6, 0))), packed_rel, n_rel // 2, True, False
    )
    new_left, new_left_state, new_rel, new_rel_state = finish(
        jobs, tail, where, (sum_a, more_a, sum_b, more_b, grad_rel, other_rel, cross_rel),
        ((left_emb[0], left_state), (relation, rel_state)), "new_left_rel",
    )
    return new_left[None], new_left_state, new_right.T[None], new_right_state, new_rel, new_rel_state[0]


def solution(mesh):
    entities = (P("row", "col", None), P("row", "col"), P("col", "row", None), P("col", "row"), P(), P())
    return jax.shard_map(
        functools.partial(body, mesh.shape["row"], mesh.shape["col"]),
        mesh=mesh,
        in_specs=entities + (P("row", "col", None),) * 3 + (P("row", "col", None, None), P("row", "col")),
        out_specs=entities,
        check_vma=False,
    )
```

```python
import functools

import jax
import jax.numpy as jnp
from jax import lax
from jax.experimental import pallas as pl
from jax.experimental.pallas import tpu as pltpu
from jax.sharding import PartitionSpec as P

CH = 1000
LANES = 128
TILE = 1024
SUB = 512
WINDOW = 128
SPAN = 256
RIGHT_CHUNK = 64
THIRDS = 64

learn_rate = 0.1
epsilon = 1e-10
bf16 = jnp.bfloat16
f32 = jnp.float32


def round_up(value, step):
    return (value + step - 1) // step * step


def to_halves(array, half_pad):
    half = array.shape[-1] // 2
    pad = [(0, 0)] * (array.ndim - 1) + [(0, half_pad - half)]
    return jnp.concatenate([jnp.pad(array[..., :half], pad), jnp.pad(array[..., half:], pad)], axis=-1)


def from_halves(array, width):
    half_pad = array.shape[-1] // 2
    return jnp.concatenate([array[..., : width // 2], array[..., half_pad : half_pad + width // 2]], axis=-1)


def bits_of(size):
    return [1 << b for b in range(size.bit_length() - 1)]


def swap(array, axis, size, bit):
    return lax.ppermute(array, axis, [(i, i ^ bit) for i in range(size)])


def tie(*arrays):
    return lax.optimization_barrier(arrays)


def gather_chunks(array, axis, size):
    for bit in reversed(bits_of(size)):
        array = jnp.concatenate([array, swap(array, axis, size, bit)], axis=0)
    return array


def reduce_chunks(array, axis, size, skip=0):
    for bit in bits_of(size)[skip:]:
        half = array.shape[0] // 2
        array = array[:half] + swap(array[half:], axis, size, bit)
    return array


def routes(size):
    rest = bits_of(size)[1:]
    turn = len(rest) // 2
    return rest, rest[turn:] + rest[:turn]


def spread(apart, route):
    place = jnp.zeros_like(apart)
    for s, bit in enumerate(reversed(route)):
        place = place | jnp.where((apart & bit) != 0, 1 << s, 0)
    return place


def owner_of(ids, share):
    owner = ((ids.astype(f32) + 0.5) * (1.0 / share)).astype(jnp.int32)
    return owner, ids - owner * share


def right_places(ids, me, size, share):
    owner, within = owner_of(ids, share)
    return spread(owner ^ me, bits_of(size)) * share + within


def left_places(ids, me, size, share):
    owner, within = owner_of(ids, share)
    apart = owner ^ me
    half = share // 2
    quarter = size // 2 * half
    first, second = (spread(apart, route) * half for route in routes(size))
    return (apart & 1) * (2 * quarter) + jnp.where(within < half, first + within, second + within + (quarter - half))


def prep_kernel(n_row, n_col, left_share, rows, where_ref, left_ref, rel_ref, right_ref, neg_ref, ids_ref, mult_ref, bound_ref, raw_ref):
    groups, _, edges = raw_ref.shape
    n_right = mult_ref.shape[2]
    n_left = left_share * n_col
    count, me_col, me_row = where_ref[0], where_ref[1], where_ref[2]
    raw_ref[...] = jnp.zeros_like(raw_ref)
    for g in range(groups):
        for k, ref in enumerate((left_ref, rel_ref, right_ref)):
            raw_ref[g, k : k + 1, :CH] = ref[0:1, g * CH : (g + 1) * CH]
        raw_ref[g, 3:4, :CH] = neg_ref[g : g + 1, :]

    def group_step(g, carry):
        raw = raw_ref[g]
        slot = lax.broadcasted_iota(jnp.int32, (1, edges), 1)
        real = slot < CH
        valid = real & (slot + g * CH < count)
        left = jnp.where(valid, left_places(raw[0:1], me_col, n_col, left_share), n_left)
        right = right_places(raw[2:3], me_row, n_row, n_right // n_row)
        neg = jnp.where(real, right_places(raw[3:4], me_row, n_row, n_right // n_row), -1)
        key = left * edges + slot
        rows_in = [key, neg, left >> 6, left & 63, raw[1:2], right >> 6, right & 63, valid.astype(jnp.int32)]
        cols = jnp.concatenate(rows_in, axis=0).T
        payload = cols.astype(f32).astype(bf16)
        rank = jnp.zeros((8, edges), jnp.int32)
        mult = jnp.zeros((8, n_right), f32)
        bound = jnp.zeros((8, LANES), jnp.int32)
        lane = lax.broadcasted_iota(jnp.int32, (LANES, LANES), 1)
        lane_start = jnp.where(lane < THIRDS, lane * rows, (lane - THIRDS) * (n_left // 3))
        lane_right = lax.broadcasted_iota(jnp.int32, (LANES, n_right), 1)
        for k in range(edges // LANES):
            part = cols[k * LANES : (k + 1) * LANES]
            less = jnp.where(part[:, 0:1] < key, 1, 0)
            rank = rank + jnp.sum(less.reshape(LANES // 8, 8, edges), axis=0)
            same = jnp.where(part[:, 1:2] == lane_right, 1.0, 0.0)
            mult = mult + jnp.sum(same.reshape(LANES // 8, 8, n_right), axis=0)
            below = jnp.where(part[:, 2:3] * 64 + part[:, 3:4] < lane_start, 1, 0)
            bound = bound + jnp.sum(below.reshape(LANES // 8, 8, LANES), axis=0)
        rank = jnp.sum(rank, axis=0, keepdims=True)
        mult_ref[g] = jnp.sum(mult, axis=0, keepdims=True)
        bound_ref[g] = jnp.sum(bound, axis=0, keepdims=True)
        moved = []
        for k in range(edges // LANES):
            place = lax.broadcasted_iota(jnp.int32, (LANES, edges), 0) + k * LANES
            moved.append(dot(jnp.where(place == rank, 1.0, 0.0).astype(bf16), payload))
        moved = jnp.concatenate(moved, axis=0).T.astype(jnp.int32)
        out = [moved[2:3] * 64 + moved[3:4], moved[4:5], moved[5:6] * 64 + moved[6:7], moved[7:8]]
        ids_ref[g] = jnp.concatenate(out + out, axis=0)
        return carry

    lax.fori_loop(0, groups, group_step, 0)


def split_two(value):
    high = value.astype(bf16)
    return high, (value - high.astype(f32)).astype(bf16)


def packed_rows(rows):
    return 3 * rows + 8


def pack(value, tail):
    rows = value.shape[0]
    lane = lax.broadcasted_iota(jnp.int32, (rows, LANES), 1)
    first, second, third, fourth = (value[:, k * LANES : (k + 1) * LANES] for k in range(4))
    mixed = jnp.where(lane < tail, second, pltpu.roll(fourth, tail, 1))
    spill = 2 * tail - LANES
    last = jnp.zeros((8, LANES), f32)
    for k in range(rows // 8):
        moved = pltpu.roll(fourth[8 * k : 8 * k + 8], (spill * k + tail) % LANES, 1)
        place = lane[:8] - spill * k
        last = jnp.where((place >= 0) & (place < spill), moved, last)
    return jnp.concatenate([first, third, mixed, last], axis=0)


def unpack(value, rows, tail):
    lane = lax.broadcasted_iota(jnp.int32, (rows, LANES), 1)
    first, third, mixed = (value[k * rows : (k + 1) * rows] for k in range(3))
    last = value[3 * rows :]
    spill = 2 * tail - LANES
    turned = pltpu.roll(third, tail, 1)
    fourth = [pltpu.roll(last, (LANES - spill * k) % LANES, 1) for k in range(rows // 8)]
    fourth = jnp.where(lane < spill, jnp.concatenate(fourth, axis=0), 0.0)
    return first, jnp.where(lane < tail, mixed, turned), jnp.where(lane < tail, turned, mixed), fourth


def finish_rows(job, tail, where_ref, grads, emb_ref, state_ref, new_ref, new_state_ref):
    parts, size, chunk, flip, turned = job
    width = emb_ref.shape[0 if turned else 1]
    totals = [sum(grads[k][start : start + size] for k, start in part) for part in parts]
    if flip:
        odd = lax.rem(where_ref[1], 2) == 1
        totals = [jnp.where(odd, totals[1], totals[0]), jnp.where(odd, totals[0], totals[1])]
    means, tiles_of = [], []
    for total in totals:
        for k in range(size // packed_rows(chunk)):
            tiles = unpack(total[k * packed_rows(chunk) : (k + 1) * packed_rows(chunk)], chunk, tail)
            squares = sum(t * t for t in tiles)
            means.append(jnp.sum(squares, axis=1, keepdims=True) / width)
            tiles_of.append(tiles)
    rows = chunk * len(means)
    mean = jnp.broadcast_to(jnp.concatenate(means, axis=0), (rows, LANES))
    state = jnp.broadcast_to(state_ref[...], (LANES, rows)).T
    accum = state + mean
    new_state_ref[...] = accum.T[0:1, :]
    rate = learn_rate / (jnp.sqrt(accum) + epsilon)
    if turned:
        tiles_of = [[jnp.concatenate(tiles, axis=0) for tiles in zip(*tiles_of)]]
        chunk = rows
    for k, tiles in enumerate(tiles_of):
        here = slice(k * chunk, (k + 1) * chunk)
        for j, tile in enumerate(tiles):
            low, high = j * LANES, min((j + 1) * LANES, width)
            if turned:
                new_ref[low:high, :] = emb_ref[low:high, :] - (rate * tile).T[: high - low]
            else:
                new_ref[here, low:high] = emb_ref[here, low:high] - (rate[here] * tile)[:, : high - low]


def finish_kernel(jobs, tail, n_grads, where_ref, *refs):
    grads, ins, outs = refs[:n_grads], refs[n_grads : n_grads + 2 * len(jobs)], refs[n_grads + 2 * len(jobs) :]
    for k, job in enumerate(jobs):
        finish_rows(job, tail, where_ref, grads, *ins[2 * k : 2 * k + 2], *outs[2 * k : 2 * k + 2])


def finish(jobs, tail, where, grads, tables, name):
    vmem = pl.BlockSpec(memory_space=pltpu.VMEM)
    shapes, operands = [], []
    for embedding, state in tables:
        operands += [embedding, state.reshape(1, -1)]
        shapes += [jax.ShapeDtypeStruct(embedding.shape, f32), jax.ShapeDtypeStruct((1, state.size), f32)]
    return pl.pallas_call(
        functools.partial(finish_kernel, jobs, tail, len(grads)),
        in_specs=[pl.BlockSpec(memory_space=pltpu.SMEM)] + [vmem] * (len(grads) + len(operands)),
        out_specs=[vmem] * len(shapes),
        out_shape=shapes,
        name=name,
    )(where, *grads, *operands)


def dot(a, b):
    return jnp.dot(a, b, preferred_element_type=f32)


def edge_kernel(
    rows, chunk, tail, where_ref, bound_ref, ids_ref, mult_ref, own_ref, other_ref, right_ref, right_t, rel_ref,
    query_ref, c_hi_ref, c_lo_ref, near_ref, far_ref,
    rel_parts, d_hi_ref, d_lo_ref, grad_rel_ref, piece_ref,
):
    step = pl.program_id(0)
    tile = query_ref.shape[0]
    groups, _, edges = ids_ref.shape
    tiles_in_group = pl.num_programs(0) // mult_ref.shape[0]
    n_rel, wide = rel_ref.shape
    half = wide // 2
    n_own, n_right = own_ref.shape[0], right_ref.shape[0]
    n_left = 2 * n_own
    rel_rows = rel_parts.shape[0]

    @pl.when(step == 0)
    def _():
        grad_rel_ref[...] = jnp.zeros_like(grad_rel_ref)
        rel_parts[...] = jnp.zeros_like(rel_parts)
        rest = rel_ref[...]
        for part in range(3):
            piece = rest.astype(bf16)
            rel_parts[part * n_rel : (part + 1) * n_rel, :] = piece
            rest = rest - piece.astype(f32)

    group = step // tiles_in_group
    start = group * CH + (step - group * tiles_in_group) * tile

    @pl.when(start >= where_ref[0])
    def _():
        for ref in (query_ref, c_hi_ref, c_lo_ref):
            ref[...] = jnp.zeros_like(ref)
        here = pl.ds(pl.multiple_of(step * tile, tile), tile)
        d_hi_ref[here, :] = jnp.zeros((tile, wide), bf16)
        d_lo_ref[here, :] = jnp.zeros((tile, wide), bf16)

    def run(spans):
        place = pl.multiple_of((step - group * tiles_in_group) * tile, tile)
        ids = ids_ref[group, :, pl.ds(place, tile)]
        all_cols = ids.T
        mult = mult_ref[group]
        absent = jnp.where(mult > 0.0, 0.0, -jnp.inf)

        def fetch(sub):
            cols = all_cols[sub * SUB : (sub + 1) * SUB]
            left_col, rel_col = cols[:, 0:1], cols[:, 1:2]
            rel_iota = lax.broadcasted_iota(jnp.int32, (SUB, rel_rows), 1) % n_rel
            rel_hot = jnp.where(rel_iota == rel_col, 1.0, 0.0).astype(bf16)
            rel_vec = dot(rel_hot, rel_parts[...])
            low, high = spans[sub]
            left_iota = lax.broadcasted_iota(jnp.int32, (SUB, high - low), 1) + low
            left_hot = jnp.where(left_iota == left_col, 1.0, 0.0).astype(bf16)
            left_vec = dot(left_hot[:, : n_own - low], own_ref[low:, :]) + dot(left_hot[:, n_own - low :], other_ref[: high - n_own, :])
            a_re, a_im = left_vec[:, :half], left_vec[:, half:]
            b_re, b_im = rel_vec[:, :half], rel_vec[:, half:]
            query = jnp.concatenate([a_re * b_re - a_im * b_im, a_re * b_im + a_im * b_re], axis=1).astype(bf16)
            query_ref[sub * SUB : (sub + 1) * SUB, :] = query
            return (a_re, a_im, b_re, b_im), dot(query, right_t[...])

        def weigh(sub, scores):
            cols = all_cols[sub * SUB : (sub + 1) * SUB]
            right_col, valid = cols[:, 2:3], cols[:, 3:4].astype(f32)
            right_iota = lax.broadcasted_iota(jnp.int32, (SUB, n_right), 1)
            is_target = right_iota == right_col
            positive = jnp.sum(jnp.where(is_target, scores, 0.0), axis=1, keepdims=True)
            masked = scores + absent
            highest = jnp.maximum(jnp.max(masked, axis=1, keepdims=True), positive)
            expo = jnp.exp(masked - highest)
            expo_pos = jnp.exp(positive - highest)
            totals = expo_pos + jnp.sum(expo * mult, axis=1, keepdims=True)
            probability = (expo * (valid / totals)).astype(bf16)
            pos_coeff = (expo_pos / totals - 1.0) * valid
            coeff = mult * probability.astype(f32) + jnp.where(is_target, pos_coeff, 0.0)
            c_hi, c_lo = split_two(coeff)
            c_hi_ref[sub * SUB : (sub + 1) * SUB, :] = c_hi
            c_lo_ref[sub * SUB : (sub + 1) * SUB, :] = c_lo
            return c_hi, c_lo

        def back(sub, parts, coeffs):
            a_re, a_im, b_re, b_im = parts
            d_query = dot(coeffs[0], right_ref[...]) + dot(coeffs[1], right_ref[...])
            g_re, g_im = d_query[:, :half], d_query[:, half:]
            d_left = jnp.concatenate([g_re * b_re + g_im * b_im, g_im * b_re - g_re * b_im], axis=1)
            d_hi, d_lo = split_two(d_left)
            here = pl.ds(pl.multiple_of(step * tile + sub * SUB, SUB), SUB)
            d_hi_ref[here, :] = d_hi
            d_lo_ref[here, :] = d_lo
            d_rel = jnp.concatenate([g_re * a_re + g_im * a_im, g_im * a_re - g_re * a_im], axis=1)
            r_hi, r_lo = split_two(d_rel)
            row_iota = lax.broadcasted_iota(jnp.int32, (n_rel, SUB), 0)
            rel_hot_t = jnp.where(row_iota == ids[1:2, sub * SUB : (sub + 1) * SUB], 1.0, 0.0).astype(bf16)
            return dot(rel_hot_t, r_hi) + dot(rel_hot_t, r_lo)

        fetched, weighed, rel_total = {}, {}, 0.0
        for turn in range(len(spans) + 2):
            if turn < len(spans):
                fetched[turn] = fetch(turn)
            if 0 <= turn - 1 < len(spans):
                weighed[turn - 1] = weigh(turn - 1, fetched[turn - 1][1])
            if 0 <= turn - 2 < len(spans):
                rel_total += back(turn - 2, fetched[turn - 2][0], weighed[turn - 2])
        grad_rel_ref[...] += rel_total

    active = start < where_ref[0]
    subs = tile // SUB
    third = n_left // 3
    if subs == 2 and tile == edges and third % LANES == 0:
        narrow = (bound_ref[group, THIRDS + 2] >= SUB) & (bound_ref[group, THIRDS + 1] <= SUB)

        @pl.when(active & narrow)
        def _():
            run(((0, 2 * third), (third, n_left)))

        active = active & jnp.logical_not(narrow)

    @pl.when(active)
    def _():
        run(((0, n_left),) * subs)

    @pl.when(step == pl.num_programs(0) - 1)
    def _():
        n_pieces = n_left // rows

        def hot_rows(g, base, at, size):
            row_iota = lax.broadcasted_iota(jnp.int32, (rows, size), 0) + base
            return jnp.where(row_iota == ids_ref[g, 0:1, pl.ds(at, size)], 1.0, 0.0).astype(bf16)

        def span(g, piece):
            return jnp.minimum(bound_ref[g, piece] // WINDOW * WINDOW, edges - SPAN)

        few = n_rel // 2
        odd = lax.rem(where_ref[1], 2)
        rel_size = packed_rows(few)
        near_ref[-rel_size:, :] = pack(grad_rel_ref[pl.ds(pl.multiple_of(odd * few, few), few), :], tail)
        far_ref[-rel_size:, :] = pack(grad_rel_ref[pl.ds(pl.multiple_of((1 - odd) * few, few), few), :], tail)

        def piece_step(piece, out_ref, shift):
            base = pl.multiple_of(piece * rows, rows)
            total = jnp.zeros((rows, wide), f32)
            for g in range(groups):
                at = pl.multiple_of(span(g, piece), WINDOW)
                hot = hot_rows(g, base, at, SPAN)
                here = pl.ds(pl.multiple_of(g * edges + at, WINDOW), SPAN)
                total = total + dot(hot, d_hi_ref[here, :]) + dot(hot, d_lo_ref[here, :])
            piece_ref[...] = total

            def rest_step(g, carry):
                def window_step(w, inner):
                    at = pl.multiple_of(w * WINDOW, WINDOW)
                    hot = hot_rows(g, base, at, WINDOW)
                    here = pl.ds(pl.multiple_of(g * edges + at, WINDOW), WINDOW)
                    piece_ref[...] += dot(hot, d_hi_ref[here, :]) + dot(hot, d_lo_ref[here, :])
                    return inner

                first = (span(g, piece) + SPAN) // WINDOW
                return lax.fori_loop(first, (bound_ref[g, piece + 1] + WINDOW - 1) // WINDOW, window_step, carry)

            lax.fori_loop(0, groups, rest_step, 0)
            size = packed_rows(chunk)
            for k in range(rows // chunk):
                there = pl.ds(pl.multiple_of((piece - shift) * (rows // chunk) * size + k * size, 8), size)
                out_ref[there, :] = pack(piece_ref[k * chunk : (k + 1) * chunk, :], tail)

        for shift, out_ref in ((0, near_ref), (n_pieces // 2, far_ref)):

            def each(k, carry, shift=shift, out_ref=out_ref):
                piece_step(k + shift, out_ref, shift)
                return carry

            lax.fori_loop(0, n_pieces // 2, each, 0, unroll=4)


def right_kernel(tail, query_ref, c_hi_ref, c_lo_ref, out_ref, total):
    step = pl.program_id(0)

    @pl.when(step == 0)
    def _():
        total[...] = jnp.zeros_like(total)

    dims = (((0,), (0,)), ((), ()))
    query = query_ref[...]
    total[...] += lax.dot_general(query, c_hi_ref[...], dims, preferred_element_type=f32) + lax.dot_general(
        query, c_lo_ref[...], dims, preferred_element_type=f32
    )

    @pl.when(step == pl.num_programs(0) - 1)
    def _():
        size = packed_rows(RIGHT_CHUNK)
        whole_sum = total[...].T
        for k in range(total.shape[1] // RIGHT_CHUNK):
            out_ref[k * size : (k + 1) * size, :] = pack(whole_sum[k * RIGHT_CHUNK : (k + 1) * RIGHT_CHUNK], tail)


def whole(shape):
    return pl.BlockSpec(shape, lambda *_: (0,) * len(shape))


def body(n_row, n_col, left_emb, left_state, right_emb, right_state, relation, rel_state, left_ids, rel_ids, right_ids, neg_ids, counts):
    width = relation.shape[1]
    half_pad = round_up(width // 2, LANES)
    wide = 2 * half_pad
    left_share, right_share = left_emb.shape[1], right_emb.shape[1]
    n_left, n_right, n_rel = left_share * n_col, right_share * n_row, relation.shape[0]
    groups = neg_ids.shape[2]
    edges = round_up(CH, TILE)
    slots = groups * edges
    tile = TILE if n_right <= SUB else SUB
    tiles = edges // tile

    smem = pl.BlockSpec(memory_space=pltpu.SMEM)
    rows = left_share * 2
    where = jnp.stack([counts[0, 0], lax.axis_index("col"), lax.axis_index("row")])

    def prepare(where, left_ids, rel_ids, right_ids, neg_ids):
        return pl.pallas_call(
            functools.partial(prep_kernel, n_row, n_col, left_share, rows),
            in_specs=[smem] + [whole((1, groups * CH))] * 3 + [whole((groups, CH))],
            out_specs=[whole((groups, 8, edges)), whole((groups, 1, n_right)), whole((groups, 1, LANES))],
            out_shape=[
                jax.ShapeDtypeStruct((groups, 8, edges), jnp.int32),
                jax.ShapeDtypeStruct((groups, 1, n_right), f32),
                jax.ShapeDtypeStruct((groups, 1, LANES), jnp.int32),
            ],
            scratch_shapes=[pltpu.VMEM((groups, 8, edges), jnp.int32)],
            cost_estimate=pl.CostEstimate(flops=16 * slots * edges, bytes_accessed=32 * slots, transcendentals=0),
            compiler_params=pltpu.CompilerParams(vmem_limit_bytes=32 << 20),
            name="prep",
        )(where, left_ids[0], rel_ids[0], right_ids[0], neg_ids[0, 0])

    rel_wide = to_halves(relation, half_pad)
    right_mine = to_halves(right_emb[0].astype(bf16), half_pad)
    mine = to_halves(left_emb[0].astype(bf16), half_pad)
    part_a, part_b = mine[: left_share // 2], mine[left_share // 2 :]
    route_a, route_b = routes(n_col)
    right_part = gather_chunks(right_mine, "row", n_row)
    for step, (bit_a, bit_b) in enumerate(zip(reversed(route_a), reversed(route_b))):
        part_a, part_b = tie(part_a, part_b)
        more_a, more_b = swap(part_a, "col", n_col, bit_a), swap(part_b, "col", n_col, bit_b)
        if step == 1:
            ids, mult, bound = prepare(*raw)
            more_a, more_b, ids, mult, bound = tie(more_a, more_b, ids, mult, bound)
        else:
            more_a, more_b = tie(more_a, more_b)
        part_a = jnp.concatenate([part_a, more_a], axis=0)
        part_b = jnp.concatenate([part_b, more_b], axis=0)
        if step == 0:
            part_a, part_b, *raw = tie(part_a, part_b, where, left_ids, rel_ids, right_ids, neg_ids)
    own = jnp.concatenate([part_a, part_b], axis=0)
    bound = bound.reshape(groups, LANES)
    own, ids, mult, bound, right_part, rel_wide = tie(own, ids, mult, bound, right_part, rel_wide)
    other = swap(own, "col", n_col, 1)

    tile_block = lambda lanes: pl.BlockSpec((tile, lanes), lambda i: (i, 0))
    chunk, tail = left_share // 2, width // 2 - LANES
    packed_half = n_left // 2 // chunk * packed_rows(chunk)
    packed_rel = packed_rows(n_rel // 2)
    query, c_hi, c_lo, near, far = pl.pallas_call(
        functools.partial(edge_kernel, rows, chunk, tail),
        grid=(groups * tiles,),
        in_specs=[
            smem,
            smem,
            whole((groups, 8, edges)),
            whole((groups, 1, n_right)),
            whole((n_left // 2, wide)),
            whole((n_left // 2, wide)),
            whole((n_right, wide)),
            whole((wide, n_right)),
            whole((n_rel, wide)),
        ],
        out_specs=[
            tile_block(wide),
            tile_block(n_right),
            tile_block(n_right),
            whole((packed_half + packed_rel, LANES)),
            whole((packed_half + packed_rel, LANES)),
        ],
        out_shape=[
            jax.ShapeDtypeStruct((slots, wide), bf16),
            jax.ShapeDtypeStruct((slots, n_right), bf16),
            jax.ShapeDtypeStruct((slots, n_right), bf16),
            jax.ShapeDtypeStruct((packed_half + packed_rel, LANES), f32),
            jax.ShapeDtypeStruct((packed_half + packed_rel, LANES), f32),
        ],
        scratch_shapes=[
            pltpu.VMEM((round_up(3 * n_rel, LANES), wide), bf16),
            pltpu.VMEM((slots, wide), bf16),
            pltpu.VMEM((slots, wide), bf16),
            pltpu.VMEM((n_rel, wide), f32),
            pltpu.VMEM((rows, wide), f32),
        ],
        compiler_params=pltpu.CompilerParams(vmem_limit_bytes=56 << 20),
        name="edges",
    )(where, bound, ids, mult, own, other, right_part, right_part.T, rel_wide)

    packed_right = n_right // RIGHT_CHUNK * packed_rows(RIGHT_CHUNK)

    def right_sum(part, query, c_hi, c_lo):
        return pl.pallas_call(
            functools.partial(right_kernel, tail),
            grid=(groups,),
            in_specs=[pl.BlockSpec((edges, wide), lambda i: (i, 0))] + [pl.BlockSpec((edges, n_right // 2), lambda i: (i, part))] * 2,
            out_specs=whole((packed_right // 2, LANES)),
            out_shape=jax.ShapeDtypeStruct((packed_right // 2, LANES), f32),
            scratch_shapes=[pltpu.VMEM((wide, n_right // 2), f32)],
            compiler_params=pltpu.CompilerParams(vmem_limit_bytes=48 << 20),
            cost_estimate=pl.CostEstimate(flops=2 * slots * wide * n_right, bytes_accessed=4 * slots * wide, transcendentals=0),
            name="right_sum",
        )(query, c_hi, c_lo)

    come, near, far_right, query, c_hi, c_lo = tie(
        swap(far, "col", n_col, 1), near, right_sum(1, query, c_hi, c_lo), query, c_hi, c_lo
    )
    half = packed_half // 2
    sum_a, sum_b = near[:half] + come[:half], near[half : 2 * half] + come[half : 2 * half]
    grad_rel = near[2 * half :] + come[2 * half :]
    sum_a, sum_b, grad_rel, query, c_hi, c_lo = tie(sum_a, sum_b, grad_rel, query, c_hi, c_lo)
    stages = len(route_a)
    carried = [route_a[k] if k % 2 else route_b[k] for k in range(1, stages)]
    alone = [("col", n_col, bit) for bit in route_a if bit not in carried]
    half = half // 2
    more_a, more_b = swap(sum_a[half:], "col", n_col, route_a[0]), swap(sum_b[half:], "col", n_col, route_b[0])
    lone = [("row", n_row, bit) for bit in bits_of(n_row)] + alone[:-1]
    for step in lone[:-1]:
        grad_rel = grad_rel + swap(grad_rel, *step)
    grad_rel, query, c_hi, c_lo = tie(grad_rel + swap(grad_rel, *lone[-1]), query, c_hi, c_lo)
    more_rel = swap(grad_rel, *alone[-1])
    come_right = swap(far_right, "row", n_row, 1)
    more_a, more_b, more_rel, near_right = tie(more_a, more_b, more_rel, right_sum(0, query, c_hi, c_lo))
    sum_a, sum_b, grad_rel, near_right = tie(sum_a[:half] + more_a, sum_b[:half] + more_b, grad_rel + more_rel, near_right)
    for stage in range(1, stages):
        half = sum_b.shape[0] // 2
        far_a, far_b = sum_a[half:], sum_b[half:]
        if stage % 2:
            far_a = jnp.concatenate([far_a, grad_rel], axis=0)
        else:
            far_b = jnp.concatenate([far_b, grad_rel], axis=0)
        more_a, more_b = swap(far_a, "col", n_col, route_a[stage]), swap(far_b, "col", n_col, route_b[stage])
        if stage == stages - 1:
            other_rel = swap(grad_rel, "col", n_col, 1)
            cross_rel = swap(grad_rel, "col", n_col, carried[-1] | 1)
            more_a, more_b, other_rel, cross_rel = tie(more_a, more_b, other_rel, cross_rel)
        if stage == 1:
            more_a, more_b, grad_right = tie(
                more_a, more_b, reduce_chunks(near_right + come_right, "row", n_row, skip=1)
            )
        elif stage == 2:
            job = (((0, 0),),), packed_right // n_row, RIGHT_CHUNK, False, True
            new_right, new_right_state = finish((job,), tail, where, (grad_right,), ((right_emb[0].T, right_state),), "new_right")
            more_a, more_b, new_right, new_right_state = tie(more_a, more_b, new_right, new_right_state)
        if stage < stages - 1:
            grad_rel = grad_rel + (more_a if stage % 2 else more_b)[half:]
            sum_a, sum_b, grad_rel = tie(sum_a[:half] + more_a[:half], sum_b[:half] + more_b[:half], grad_rel)
    jobs = (
        (((0, 0), (1, 0)), ((2, 0), (3, 0))), half, chunk, False, False
    ), (
        (((4, 0), (1 if stage % 2 else 3, half)), ((5, 0), (6, 0))), packed_rel, n_rel // 2, True, False
    )
    new_left, new_left_state, new_rel, new_rel_state = finish(
        jobs, tail, where, (sum_a, more_a, sum_b, more_b, grad_rel, other_rel, cross_rel),
        ((left_emb[0], left_state), (relation, rel_state)), "new_left_rel",
    )
    return new_left[None], new_left_state, new_right.T[None], new_right_state, new_rel, new_rel_state[0]


def solution(mesh):
    entities = (P("row", "col", None), P("row", "col"), P("col", "row", None), P("col", "row"), P(), P())
    return jax.shard_map(
        functools.partial(body, mesh.shape["row"], mesh.shape["col"]),
        mesh=mesh,
        in_specs=entities + (P("row", "col", None),) * 3 + (P("row", "col", None, None), P("row", "col")),
        out_specs=entities,
        check_vma=False,
    )
```

```python
import functools

import jax
import jax.numpy as jnp
from jax import lax
from jax.experimental import pallas as pl
from jax.experimental.pallas import tpu as pltpu
from jax.sharding import PartitionSpec as P

CH = 1000
LANES = 128
TILE = 1024
SUB = 512
WINDOW = 128
SPAN = 256
RIGHT_CHUNK = 64
THIRDS = 64

learn_rate = 0.1
epsilon = 1e-10
bf16 = jnp.bfloat16
f32 = jnp.float32


def round_up(value, step):
    return (value + step - 1) // step * step


def to_halves(array, half_pad):
    half = array.shape[-1] // 2
    pad = [(0, 0)] * (array.ndim - 1) + [(0, half_pad - half)]
    return jnp.concatenate([jnp.pad(array[..., :half], pad), jnp.pad(array[..., half:], pad)], axis=-1)


def from_halves(array, width):
    half_pad = array.shape[-1] // 2
    return jnp.concatenate([array[..., : width // 2], array[..., half_pad : half_pad + width // 2]], axis=-1)


def bits_of(size):
    return [1 << b for b in range(size.bit_length() - 1)]


def swap(array, axis, size, bit):
    return lax.ppermute(array, axis, [(i, i ^ bit) for i in range(size)])


def tie(*arrays):
    return lax.optimization_barrier(arrays)


def gather_chunks(array, axis, size):
    for bit in reversed(bits_of(size)):
        array = jnp.concatenate([array, swap(array, axis, size, bit)], axis=0)
    return array


def reduce_chunks(array, axis, size, skip=0):
    for bit in bits_of(size)[skip:]:
        half = array.shape[0] // 2
        array = array[:half] + swap(array[half:], axis, size, bit)
    return array


def routes(size):
    rest = bits_of(size)[1:]
    turn = len(rest) // 2
    return rest, rest[turn:] + rest[:turn]


def spread(apart, route):
    place = jnp.zeros_like(apart)
    for s, bit in enumerate(reversed(route)):
        place = place | jnp.where((apart & bit) != 0, 1 << s, 0)
    return place


def owner_of(ids, share):
    owner = ((ids.astype(f32) + 0.5) * (1.0 / share)).astype(jnp.int32)
    return owner, ids - owner * share


def right_places(ids, me, size, share):
    owner, within = owner_of(ids, share)
    return spread(owner ^ me, bits_of(size)) * share + within


def left_places(ids, me, size, share):
    owner, within = owner_of(ids, share)
    apart = owner ^ me
    half = share // 2
    quarter = size // 2 * half
    first, second = (spread(apart, route) * half for route in routes(size))
    return (apart & 1) * (2 * quarter) + jnp.where(within < half, first + within, second + within + (quarter - half))


def prep_kernel(n_row, n_col, left_share, rows, where_ref, left_ref, rel_ref, right_ref, neg_ref, ids_ref, mult_ref, bound_ref, raw_ref):
    groups, _, edges = raw_ref.shape
    n_right = mult_ref.shape[2]
    n_left = left_share * n_col
    count, me_col, me_row = where_ref[0], where_ref[1], where_ref[2]
    raw_ref[...] = jnp.zeros_like(raw_ref)
    for g in range(groups):
        for k, ref in enumerate((left_ref, rel_ref, right_ref)):
            raw_ref[g, k : k + 1, :CH] = ref[0:1, g * CH : (g + 1) * CH]
        raw_ref[g, 3:4, :CH] = neg_ref[g : g + 1, :]

    def group_step(g, carry):
        raw = raw_ref[g]
        slot = lax.broadcasted_iota(jnp.int32, (1, edges), 1)
        real = slot < CH
        valid = real & (slot + g * CH < count)
        left = jnp.where(valid, left_places(raw[0:1], me_col, n_col, left_share), n_left)
        right = right_places(raw[2:3], me_row, n_row, n_right // n_row)
        neg = jnp.where(real, right_places(raw[3:4], me_row, n_row, n_right // n_row), -1)
        key = left * edges + slot
        rows_in = [key, neg, left >> 6, left & 63, raw[1:2], right >> 6, right & 63, valid.astype(jnp.int32)]
        cols = jnp.concatenate(rows_in, axis=0).T
        payload = cols.astype(f32).astype(bf16)
        rank = jnp.zeros((8, edges), jnp.int32)
        mult = jnp.zeros((8, n_right), f32)
        bound = jnp.zeros((8, LANES), jnp.int32)
        lane = lax.broadcasted_iota(jnp.int32, (LANES, LANES), 1)
        lane_start = jnp.where(lane < THIRDS, lane * rows, (lane - THIRDS) * (n_left // 3))
        lane_right = lax.broadcasted_iota(jnp.int32, (LANES, n_right), 1)
        for k in range(edges // LANES):
            part = cols[k * LANES : (k + 1) * LANES]
            less = jnp.where(part[:, 0:1] < key, 1, 0)
            rank = rank + jnp.sum(less.reshape(LANES // 8, 8, edges), axis=0)
            same = jnp.where(part[:, 1:2] == lane_right, 1.0, 0.0)
            mult = mult + jnp.sum(same.reshape(LANES // 8, 8, n_right), axis=0)
            below = jnp.where(part[:, 2:3] * 64 + part[:, 3:4] < lane_start, 1, 0)
            bound = bound + jnp.sum(below.reshape(LANES // 8, 8, LANES), axis=0)
        rank = jnp.sum(rank, axis=0, keepdims=True)
        mult_ref[g] = jnp.sum(mult, axis=0, keepdims=True)
        bound_ref[g] = jnp.sum(bound, axis=0, keepdims=True)
        moved = []
        for k in range(edges // LANES):
            place = lax.broadcasted_iota(jnp.int32, (LANES, edges), 0) + k * LANES
            moved.append(dot(jnp.where(place == rank, 1.0, 0.0).astype(bf16), payload))
        moved = jnp.concatenate(moved, axis=0).T.astype(jnp.int32)
        out = [moved[2:3] * 64 + moved[3:4], moved[4:5], moved[5:6] * 64 + moved[6:7], moved[7:8]]
        ids_ref[g] = jnp.concatenate(out + out, axis=0)
        return carry

    lax.fori_loop(0, groups, group_step, 0)


def split_two(value):
    high = value.astype(bf16)
    return high, (value - high.astype(f32)).astype(bf16)


def packed_rows(rows):
    return 3 * rows + 8


def pack(value, tail):
    rows = value.shape[0]
    lane = lax.broadcasted_iota(jnp.int32, (rows, LANES), 1)
    first, second, third, fourth = (value[:, k * LANES : (k + 1) * LANES] for k in range(4))
    mixed = jnp.where(lane < tail, second, pltpu.roll(fourth, tail, 1))
    spill = 2 * tail - LANES
    last = jnp.zeros((8, LANES), f32)
    for k in range(rows // 8):
        moved = pltpu.roll(fourth[8 * k : 8 * k + 8], (spill * k + tail) % LANES, 1)
        place = lane[:8] - spill * k
        last = jnp.where((place >= 0) & (place < spill), moved, last)
    return jnp.concatenate([first, third, mixed, last], axis=0)


def unpack(value, rows, tail):
    lane = lax.broadcasted_iota(jnp.int32, (rows, LANES), 1)
    first, third, mixed = (value[k * rows : (k + 1) * rows] for k in range(3))
    last = value[3 * rows :]
    spill = 2 * tail - LANES
    turned = pltpu.roll(third, tail, 1)
    fourth = [pltpu.roll(last, (LANES - spill * k) % LANES, 1) for k in range(rows // 8)]
    fourth = jnp.where(lane < spill, jnp.concatenate(fourth, axis=0), 0.0)
    return first, jnp.where(lane < tail, mixed, turned), jnp.where(lane < tail, turned, mixed), fourth


def finish_rows(job, tail, where_ref, grads, emb_ref, state_ref, new_ref, new_state_ref):
    parts, size, chunk, flip, turned = job
    width = emb_ref.shape[0 if turned else 1]
    totals = [sum(grads[k][start : start + size] for k, start in part) for part in parts]
    if flip:
        odd = lax.rem(where_ref[1], 2) == 1
        totals = [jnp.where(odd, totals[1], totals[0]), jnp.where(odd, totals[0], totals[1])]
    means, tiles_of = [], []
    for total in totals:
        for k in range(size // packed_rows(chunk)):
            tiles = unpack(total[k * packed_rows(chunk) : (k + 1) * packed_rows(chunk)], chunk, tail)
            squares = sum(t * t for t in tiles)
            means.append(jnp.sum(squares, axis=1, keepdims=True) / width)
            tiles_of.append(tiles)
    rows = chunk * len(means)
    mean = jnp.broadcast_to(jnp.concatenate(means, axis=0), (rows, LANES))
    state = jnp.broadcast_to(state_ref[...], (LANES, rows)).T
    accum = state + mean
    new_state_ref[...] = accum.T[0:1, :]
    rate = learn_rate / (jnp.sqrt(accum) + epsilon)
    if turned:
        tiles_of = [[jnp.concatenate(tiles, axis=0) for tiles in zip(*tiles_of)]]
        chunk = rows
    for k, tiles in enumerate(tiles_of):
        here = slice(k * chunk, (k + 1) * chunk)
        for j, tile in enumerate(tiles):
            low, high = j * LANES, min((j + 1) * LANES, width)
            if turned:
                new_ref[low:high, :] = emb_ref[low:high, :] - (rate * tile).T[: high - low]
            else:
                new_ref[here, low:high] = emb_ref[here, low:high] - (rate[here] * tile)[:, : high - low]


def finish_kernel(jobs, tail, n_grads, where_ref, *refs):
    grads, ins, outs = refs[:n_grads], refs[n_grads : n_grads + 2 * len(jobs)], refs[n_grads + 2 * len(jobs) :]
    for k, job in enumerate(jobs):
        finish_rows(job, tail, where_ref, grads, *ins[2 * k : 2 * k + 2], *outs[2 * k : 2 * k + 2])


def finish(jobs, tail, where, grads, tables, name):
    vmem = pl.BlockSpec(memory_space=pltpu.VMEM)
    shapes, operands = [], []
    for embedding, state in tables:
        operands += [embedding, state.reshape(1, -1)]
        shapes += [jax.ShapeDtypeStruct(embedding.shape, f32), jax.ShapeDtypeStruct((1, state.size), f32)]
    return pl.pallas_call(
        functools.partial(finish_kernel, jobs, tail, len(grads)),
        in_specs=[pl.BlockSpec(memory_space=pltpu.SMEM)] + [vmem] * (len(grads) + len(operands)),
        out_specs=[vmem] * len(shapes),
        out_shape=shapes,
        name=name,
    )(where, *grads, *operands)


def dot(a, b):
    return jnp.dot(a, b, preferred_element_type=f32)


def edge_kernel(
    rows, chunk, tail, where_ref, bound_ref, ids_ref, mult_ref, own_ref, other_ref, right_ref, right_t, rel_ref,
    query_ref, c_hi_ref, c_lo_ref, near_ref, far_ref,
    rel_parts, d_hi_ref, d_lo_ref, grad_rel_ref, piece_ref,
):
    step = pl.program_id(0)
    tile = query_ref.shape[0]
    groups, _, edges = ids_ref.shape
    tiles_in_group = pl.num_programs(0) // mult_ref.shape[0]
    n_rel, wide = rel_ref.shape
    half = wide // 2
    n_own, n_right = own_ref.shape[0], right_ref.shape[0]
    n_left = 2 * n_own
    rel_rows = rel_parts.shape[0]

    @pl.when(step == 0)
    def _():
        grad_rel_ref[...] = jnp.zeros_like(grad_rel_ref)
        rel_parts[...] = jnp.zeros_like(rel_parts)
        rest = rel_ref[...]
        for part in range(3):
            piece = rest.astype(bf16)
            rel_parts[part * n_rel : (part + 1) * n_rel, :] = piece
            rest = rest - piece.astype(f32)

    group = step // tiles_in_group
    start = group * CH + (step - group * tiles_in_group) * tile

    @pl.when(start >= where_ref[0])
    def _():
        for ref in (query_ref, c_hi_ref, c_lo_ref):
            ref[...] = jnp.zeros_like(ref)
        here = pl.ds(pl.multiple_of(step * tile, tile), tile)
        d_hi_ref[here, :] = jnp.zeros((tile, wide), bf16)
        d_lo_ref[here, :] = jnp.zeros((tile, wide), bf16)

    def run(spans):
        place = pl.multiple_of((step - group * tiles_in_group) * tile, tile)
        ids = ids_ref[group, :, pl.ds(place, tile)]
        all_cols = ids.T
        mult = mult_ref[group]
        absent = jnp.where(mult > 0.0, 0.0, -jnp.inf)

        def fetch(sub):
            cols = all_cols[sub * SUB : (sub + 1) * SUB]
            left_col, rel_col = cols[:, 0:1], cols[:, 1:2]
            rel_iota = lax.broadcasted_iota(jnp.int32, (SUB, rel_rows), 1) % n_rel
            rel_hot = jnp.where(rel_iota == rel_col, 1.0, 0.0).astype(bf16)
            rel_vec = dot(rel_hot, rel_parts[...])
            low, high = spans[sub]
            left_iota = lax.broadcasted_iota(jnp.int32, (SUB, high - low), 1) + low
            left_hot = jnp.where(left_iota == left_col, 1.0, 0.0).astype(bf16)
            left_vec = dot(left_hot[:, : n_own - low], own_ref[low:, :]) + dot(left_hot[:, n_own - low :], other_ref[: high - n_own, :])
            a_re, a_im = left_vec[:, :half], left_vec[:, half:]
            b_re, b_im = rel_vec[:, :half], rel_vec[:, half:]
            query = jnp.concatenate([a_re * b_re - a_im * b_im, a_re * b_im + a_im * b_re], axis=1).astype(bf16)
            query_ref[sub * SUB : (sub + 1) * SUB, :] = query
            return (a_re, a_im, b_re, b_im), dot(query, right_t[...])

        def weigh(sub, scores):
            cols = all_cols[sub * SUB : (sub + 1) * SUB]
            right_col, valid = cols[:, 2:3], cols[:, 3:4].astype(f32)
            right_iota = lax.broadcasted_iota(jnp.int32, (SUB, n_right), 1)
            is_target = right_iota == right_col
            positive = jnp.sum(jnp.where(is_target, scores, 0.0), axis=1, keepdims=True)
            masked = scores + absent
            highest = jnp.maximum(jnp.max(masked, axis=1, keepdims=True), positive)
            expo = jnp.exp(masked - highest)
            expo_pos = jnp.exp(positive - highest)
            totals = expo_pos + jnp.sum(expo * mult, axis=1, keepdims=True)
            probability = (expo * (valid / totals)).astype(bf16)
            pos_coeff = (expo_pos / totals - 1.0) * valid
            coeff = mult * probability.astype(f32) + jnp.where(is_target, pos_coeff, 0.0)
            c_hi, c_lo = split_two(coeff)
            c_hi_ref[sub * SUB : (sub + 1) * SUB, :] = c_hi
            c_lo_ref[sub * SUB : (sub + 1) * SUB, :] = c_lo
            return c_hi, c_lo

        def back(sub, parts, coeffs):
            a_re, a_im, b_re, b_im = parts
            d_query = dot(coeffs[0], right_ref[...]) + dot(coeffs[1], right_ref[...])
            g_re, g_im = d_query[:, :half], d_query[:, half:]
            d_left = jnp.concatenate([g_re * b_re + g_im * b_im, g_im * b_re - g_re * b_im], axis=1)
            d_hi, d_lo = split_two(d_left)
            here = pl.ds(pl.multiple_of(step * tile + sub * SUB, SUB), SUB)
            d_hi_ref[here, :] = d_hi
            d_lo_ref[here, :] = d_lo
            d_rel = jnp.concatenate([g_re * a_re + g_im * a_im, g_im * a_re - g_re * a_im], axis=1)
            r_hi, r_lo = split_two(d_rel)
            row_iota = lax.broadcasted_iota(jnp.int32, (n_rel, SUB), 0)
            rel_hot_t = jnp.where(row_iota == ids[1:2, sub * SUB : (sub + 1) * SUB], 1.0, 0.0).astype(bf16)
            return dot(rel_hot_t, r_hi) + dot(rel_hot_t, r_lo)

        fetched, weighed, rel_total = {}, {}, 0.0
        for turn in range(len(spans) + 2):
            if 0 <= turn - 1 < len(spans):
                weighed[turn - 1] = weigh(turn - 1, fetched[turn - 1][1])
            if turn < len(spans):
                fetched[turn] = fetch(turn)
            if 0 <= turn - 2 < len(spans):
                rel_total += back(turn - 2, fetched[turn - 2][0], weighed[turn - 2])

        grad_rel_ref[...] += rel_total

    active = start < where_ref[0]
    subs = tile // SUB
    third = n_left // 3
    if subs == 2 and tile == edges and third % LANES == 0:
        narrow = (bound_ref[group, THIRDS + 2] >= SUB) & (bound_ref[group, THIRDS + 1] <= SUB)

        @pl.when(active & narrow)
        def _():
            run(((0, 2 * third), (third, n_left)))

        active = active & jnp.logical_not(narrow)

    @pl.when(active)
    def _():
        run(((0, n_left),) * subs)

    @pl.when(step == pl.num_programs(0) - 1)
    def _():
        n_pieces = n_left // rows

        def hot_rows(g, base, at, size):
            row_iota = lax.broadcasted_iota(jnp.int32, (rows, size), 0) + base
            return jnp.where(row_iota == ids_ref[g, 0:1, pl.ds(at, size)], 1.0, 0.0).astype(bf16)

        def span(g, piece):
            return jnp.minimum(bound_ref[g, piece] // WINDOW * WINDOW, edges - SPAN)

        few = n_rel // 2
        odd = lax.rem(where_ref[1], 2)
        rel_size = packed_rows(few)
        near_ref[-rel_size:, :] = pack(grad_rel_ref[pl.ds(pl.multiple_of(odd * few, few), few), :], tail)
        far_ref[-rel_size:, :] = pack(grad_rel_ref[pl.ds(pl.multiple_of((1 - odd) * few, few), few), :], tail)

        def piece_step(piece, out_ref, shift):
            base = pl.multiple_of(piece * rows, rows)
            total = jnp.zeros((rows, wide), f32)
            for g in range(groups):
                at = pl.multiple_of(span(g, piece), WINDOW)
                hot = hot_rows(g, base, at, SPAN)
                here = pl.ds(pl.multiple_of(g * edges + at, WINDOW), SPAN)
                total = total + dot(hot, d_hi_ref[here, :]) + dot(hot, d_lo_ref[here, :])
            piece_ref[...] = total

            def rest_step(g, carry):
                def window_step(w, inner):
                    at = pl.multiple_of(w * WINDOW, WINDOW)
                    hot = hot_rows(g, base, at, WINDOW)
                    here = pl.ds(pl.multiple_of(g * edges + at, WINDOW), WINDOW)
                    piece_ref[...] += dot(hot, d_hi_ref[here, :]) + dot(hot, d_lo_ref[here, :])
                    return inner

                first = (span(g, piece) + SPAN) // WINDOW
                return lax.fori_loop(first, (bound_ref[g, piece + 1] + WINDOW - 1) // WINDOW, window_step, carry)

            more = bound_ref[0, piece + 1] > span(0, piece) + SPAN
            for g in range(1, groups):
                more = more | (bound_ref[g, piece + 1] > span(g, piece) + SPAN)

            @pl.when(more)
            def _():
                lax.fori_loop(0, groups, rest_step, 0)

            size = packed_rows(chunk)
            for k in range(rows // chunk):
                there = pl.ds(pl.multiple_of((piece - shift) * (rows // chunk) * size + k * size, 8), size)
                out_ref[there, :] = pack(piece_ref[k * chunk : (k + 1) * chunk, :], tail)

        for shift, out_ref in ((0, near_ref), (n_pieces // 2, far_ref)):

            def each(k, carry, shift=shift, out_ref=out_ref):
                piece_step(k + shift, out_ref, shift)
                return carry

            lax.fori_loop(0, n_pieces // 2, each, 0, unroll=4)


def right_kernel(tail, query_ref, c_hi_ref, c_lo_ref, out_ref, total):
    step = pl.program_id(0)

    @pl.when(step == 0)
    def _():
        total[...] = jnp.zeros_like(total)

    dims = (((0,), (0,)), ((), ()))
    query = query_ref[...]
    total[...] += lax.dot_general(query, c_hi_ref[...], dims, preferred_element_type=f32) + lax.dot_general(
        query, c_lo_ref[...], dims, preferred_element_type=f32
    )

    @pl.when(step == pl.num_programs(0) - 1)
    def _():
        size = packed_rows(RIGHT_CHUNK)
        whole_sum = total[...].T
        for k in range(total.shape[1] // RIGHT_CHUNK):
            out_ref[k * size : (k + 1) * size, :] = pack(whole_sum[k * RIGHT_CHUNK : (k + 1) * RIGHT_CHUNK], tail)


def whole(shape):
    return pl.BlockSpec(shape, lambda *_: (0,) * len(shape))


def body(n_row, n_col, left_emb, left_state, right_emb, right_state, relation, rel_state, left_ids, rel_ids, right_ids, neg_ids, counts):
    width = relation.shape[1]
    half_pad = round_up(width // 2, LANES)
    wide = 2 * half_pad
    left_share, right_share = left_emb.shape[1], right_emb.shape[1]
    n_left, n_right, n_rel = left_share * n_col, right_share * n_row, relation.shape[0]
    groups = neg_ids.shape[2]
    edges = round_up(CH, TILE)
    slots = groups * edges
    tile = TILE if n_right <= SUB else SUB
    tiles = edges // tile

    smem = pl.BlockSpec(memory_space=pltpu.SMEM)
    rows = left_share * 2
    where = jnp.stack([counts[0, 0], lax.axis_index("col"), lax.axis_index("row")])

    def prepare(where, left_ids, rel_ids, right_ids, neg_ids):
        return pl.pallas_call(
            functools.partial(prep_kernel, n_row, n_col, left_share, rows),
            in_specs=[smem] + [whole((1, groups * CH))] * 3 + [whole((groups, CH))],
            out_specs=[whole((groups, 8, edges)), whole((groups, 1, n_right)), whole((groups, 1, LANES))],
            out_shape=[
                jax.ShapeDtypeStruct((groups, 8, edges), jnp.int32),
                jax.ShapeDtypeStruct((groups, 1, n_right), f32),
                jax.ShapeDtypeStruct((groups, 1, LANES), jnp.int32),
            ],
            scratch_shapes=[pltpu.VMEM((groups, 8, edges), jnp.int32)],
            cost_estimate=pl.CostEstimate(flops=16 * slots * edges, bytes_accessed=32 * slots, transcendentals=0),
            compiler_params=pltpu.CompilerParams(vmem_limit_bytes=32 << 20),
            name="prep",
        )(where, left_ids[0], rel_ids[0], right_ids[0], neg_ids[0, 0])

    rel_wide = to_halves(relation, half_pad)
    right_mine = to_halves(right_emb[0].astype(bf16), half_pad)
    mine = to_halves(left_emb[0].astype(bf16), half_pad)
    part_a, part_b = mine[: left_share // 2], mine[left_share // 2 :]
    route_a, route_b = routes(n_col)
    right_part = gather_chunks(right_mine, "row", n_row)
    for step, (bit_a, bit_b) in enumerate(zip(reversed(route_a), reversed(route_b))):
        part_a, part_b = tie(part_a, part_b)
        more_a, more_b = swap(part_a, "col", n_col, bit_a), swap(part_b, "col", n_col, bit_b)
        if step == 1:
            ids, mult, bound = prepare(*raw)
            more_a, more_b, ids, mult, bound = tie(more_a, more_b, ids, mult, bound)
        else:
            more_a, more_b = tie(more_a, more_b)
        part_a = jnp.concatenate([part_a, more_a], axis=0)
        part_b = jnp.concatenate([part_b, more_b], axis=0)
        if step == 0:
            part_a, part_b, *raw = tie(part_a, part_b, where, left_ids, rel_ids, right_ids, neg_ids)
    own = jnp.concatenate([part_a, part_b], axis=0)
    bound = bound.reshape(groups, LANES)
    own, ids, mult, bound, right_part, rel_wide = tie(own, ids, mult, bound, right_part, rel_wide)
    other = swap(own, "col", n_col, 1)

    tile_block = lambda lanes: pl.BlockSpec((tile, lanes), lambda i: (i, 0))
    chunk, tail = left_share // 2, width // 2 - LANES
    packed_half = n_left // 2 // chunk * packed_rows(chunk)
    packed_rel = packed_rows(n_rel // 2)
    query, c_hi, c_lo, near, far = pl.pallas_call(
        functools.partial(edge_kernel, rows, chunk, tail),
        grid=(groups * tiles,),
        in_specs=[
            smem,
            smem,
            whole((groups, 8, edges)),
            whole((groups, 1, n_right)),
            whole((n_left // 2, wide)),
            whole((n_left // 2, wide)),
            whole((n_right, wide)),
            whole((wide, n_right)),
            whole((n_rel, wide)),
        ],
        out_specs=[
            tile_block(wide),
            tile_block(n_right),
            tile_block(n_right),
            whole((packed_half + packed_rel, LANES)),
            whole((packed_half + packed_rel, LANES)),
        ],
        out_shape=[
            jax.ShapeDtypeStruct((slots, wide), bf16),
            jax.ShapeDtypeStruct((slots, n_right), bf16),
            jax.ShapeDtypeStruct((slots, n_right), bf16),
            jax.ShapeDtypeStruct((packed_half + packed_rel, LANES), f32),
            jax.ShapeDtypeStruct((packed_half + packed_rel, LANES), f32),
        ],
        scratch_shapes=[
            pltpu.VMEM((round_up(3 * n_rel, LANES), wide), bf16),
            pltpu.VMEM((slots, wide), bf16),
            pltpu.VMEM((slots, wide), bf16),
            pltpu.VMEM((n_rel, wide), f32),
            pltpu.VMEM((rows, wide), f32),
        ],
        compiler_params=pltpu.CompilerParams(vmem_limit_bytes=56 << 20),
        name="edges",
    )(where, bound, ids, mult, own, other, right_part, right_part.T, rel_wide)

    packed_right = n_right // RIGHT_CHUNK * packed_rows(RIGHT_CHUNK)

    def right_sum(part, query, c_hi, c_lo):
        return pl.pallas_call(
            functools.partial(right_kernel, tail),
            grid=(groups,),
            in_specs=[pl.BlockSpec((edges, wide), lambda i: (i, 0))] + [pl.BlockSpec((edges, n_right // 2), lambda i: (i, part))] * 2,
            out_specs=whole((packed_right // 2, LANES)),
            out_shape=jax.ShapeDtypeStruct((packed_right // 2, LANES), f32),
            scratch_shapes=[pltpu.VMEM((wide, n_right // 2), f32)],
            compiler_params=pltpu.CompilerParams(vmem_limit_bytes=48 << 20),
            cost_estimate=pl.CostEstimate(flops=2 * slots * wide * n_right, bytes_accessed=4 * slots * wide, transcendentals=0),
            name="right_sum",
        )(query, c_hi, c_lo)

    come, near, far_right, query, c_hi, c_lo = tie(
        swap(far, "col", n_col, 1), near, right_sum(1, query, c_hi, c_lo), query, c_hi, c_lo
    )
    half = packed_half // 2
    sum_a, sum_b = near[:half] + come[:half], near[half : 2 * half] + come[half : 2 * half]
    grad_rel = near[2 * half :] + come[2 * half :]
    sum_a, sum_b, grad_rel, query, c_hi, c_lo = tie(sum_a, sum_b, grad_rel, query, c_hi, c_lo)
    stages = len(route_a)
    carried = [route_a[k] if k % 2 else route_b[k] for k in range(1, stages)]
    alone = [("col", n_col, bit) for bit in route_a if bit not in carried]
    half = half // 2
    more_a, more_b = swap(sum_a[half:], "col", n_col, route_a[0]), swap(sum_b[half:], "col", n_col, route_b[0])
    lone = [("row", n_row, bit) for bit in bits_of(n_row)] + alone[:-1]
    for step in lone[:-1]:
        grad_rel = grad_rel + swap(grad_rel, *step)
    grad_rel, query, c_hi, c_lo = tie(grad_rel + swap(grad_rel, *lone[-1]), query, c_hi, c_lo)
    more_rel = swap(grad_rel, *alone[-1])
    come_right = swap(far_right, "row", n_row, 1)
    more_a, more_b, more_rel, near_right = tie(more_a, more_b, more_rel, right_sum(0, query, c_hi, c_lo))
    sum_a, sum_b, grad_rel, near_right = tie(sum_a[:half] + more_a, sum_b[:half] + more_b, grad_rel + more_rel, near_right)
    for stage in range(1, stages):
        half = sum_b.shape[0] // 2
        far_a, far_b = sum_a[half:], sum_b[half:]
        if stage % 2:
            far_a = jnp.concatenate([far_a, grad_rel], axis=0)
        else:
            far_b = jnp.concatenate([far_b, grad_rel], axis=0)
        more_a, more_b = swap(far_a, "col", n_col, route_a[stage]), swap(far_b, "col", n_col, route_b[stage])
        if stage == stages - 1:
            other_rel = swap(grad_rel, "col", n_col, 1)
            cross_rel = swap(grad_rel, "col", n_col, carried[-1] | 1)
            more_a, more_b, other_rel, cross_rel = tie(more_a, more_b, other_rel, cross_rel)
        if stage == 1:
            more_a, more_b, grad_right = tie(
                more_a, more_b, reduce_chunks(near_right + come_right, "row", n_row, skip=1)
            )
        elif stage == 2:
            job = (((0, 0),),), packed_right // n_row, RIGHT_CHUNK, False, True
            new_right, new_right_state = finish((job,), tail, where, (grad_right,), ((right_emb[0].T, right_state),), "new_right")
            more_a, more_b, new_right, new_right_state = tie(more_a, more_b, new_right, new_right_state)
        if stage < stages - 1:
            grad_rel = grad_rel + (more_a if stage % 2 else more_b)[half:]
            sum_a, sum_b, grad_rel = tie(sum_a[:half] + more_a[:half], sum_b[:half] + more_b[:half], grad_rel)
    jobs = (
        (((0, 0), (1, 0)), ((2, 0), (3, 0))), half, chunk, False, False
    ), (
        (((4, 0), (1 if stage % 2 else 3, half)), ((5, 0), (6, 0))), packed_rel, n_rel // 2, True, False
    )
    new_left, new_left_state, new_rel, new_rel_state = finish(
        jobs, tail, where, (sum_a, more_a, sum_b, more_b, grad_rel, other_rel, cross_rel),
        ((left_emb[0], left_state), (relation, rel_state)), "new_left_rel",
    )
    return new_left[None], new_left_state, new_right.T[None], new_right_state, new_rel, new_rel_state[0]


def solution(mesh):
    entities = (P("row", "col", None), P("row", "col"), P("col", "row", None), P("col", "row"), P(), P())
    return jax.shard_map(
        functools.partial(body, mesh.shape["row"], mesh.shape["col"]),
        mesh=mesh,
        in_specs=entities + (P("row", "col", None),) * 3 + (P("row", "col", None, None), P("row", "col")),
        out_specs=entities,
        check_vma=False,
    )
```
